512 devices in a mesh: tile: 128 (over z, x, core), view: 4 (over y).
Axes of the slice: x: 4, y: 4, z: 16, core: 2. Of those that a mesh axis runs over, the one named last changes fastest.
Arguments:
- gaussians: float32 [59, 524288], P(None, ('tile', 'view')), as said below
- camera: float32 [4, 12], replicated, as said below
- send_index: int32 [512, 2, 128, 4], P(('tile', 'view')), may hold values from -1 to 1023, as said below
- tile_ids: int32 [4, 128, 2], P('view', 'tile'), may hold values from 0 to 32399, as said below
- tile_lists: int32 [4, 128, 2, 256], P('view', 'tile'), may hold values from 0 to 1023, as said below
- tile_lengths: int32 [4, 128, 2], P('view', 'tile'), may hold values from 32 to 256
- pixel_grad: float32 [3, 4, 65536], P(None, 'view', 'tile'), may hold values from -6 to 6
Outputs:
- image: float32 [3, 4, 65536], P(None, 'view', 'tile')
- gaussian_grads: float32 [59, 524288], P(None, ('tile', 'view'))
The draws below stay inside these ranges and needn't reach their ends.
Inputs may be any that keep to these rules, and one draw needn't show every extreme that they name: `send_index`: entry [s, c, t, v] is the column within device s's 1024 Gaussians of the c-th Gaussian that s sends to device t * 4 + v, or -1; the sent ones to one device form a prefix in c; the non-negative entries of one s are distinct; every device receives 2 Gaussians from at least one source. `tile_lists`: entries are slots c * 512 + s of Gaussians actually sent to that device; each sent slot stands exactly once among the used entries of the device's tiles; used entries are ordered by increasing depth z; entries past the length repeat used entries of the same tile. `tile_ids`: tiles are numbered row by row in a frame 240 tiles wide and 135 high; the tiles of one view are distinct. `gaussians`: every Gaussian that is sent lies at depth z between 2 and 8 in front of its destination's camera; g[6] lies in [0.5, 1.5]; opacity logits are at most -1. `camera`: each row holds a rotation matrix and a translation.
All inputs are finite; a program needn't handle non-finite values.
Results may differ from the reference program's by a relative error of at most 0.0009.
Values sent between devices are 32-bit elements; how exact they have to be, the bound alone decides.
A program may use at most 64 MiB of HBM per device.

```python
import jax
import jax.numpy as jnp
from jax import lax

G_DEV = 1024
TILES_DEV = 2
K = 256
VIEWS = 4
PIX = 65536
N_TILE = 128
N_VIEW = 4


def camera_rows(key):
    key = jax.random.fold_in(key, 101)
    keys = jax.random.split(key, 3)
    yaw = jax.random.uniform(keys[0], (N_VIEW,), jnp.float32, -0.6, 0.6)
    pitch = jax.random.uniform(keys[1], (N_VIEW,), jnp.float32, -0.3, 0.3)
    shift = jax.random.uniform(keys[2], (N_VIEW, 3), jnp.float32, -1.0, 1.0)
    cos_yaw = jnp.cos(yaw)
    sin_yaw = jnp.sin(yaw)
    cos_pitch = jnp.cos(pitch)
    sin_pitch = jnp.sin(pitch)
    zeros = jnp.zeros_like(yaw)
    entries = [cos_yaw, zeros, sin_yaw, sin_pitch * sin_yaw, cos_pitch, -sin_pitch * cos_yaw, -cos_pitch * sin_yaw, sin_pitch, cos_pitch * cos_yaw, shift[:, 0], shift[:, 1], shift[:, 2]]
    return jnp.stack(entries, axis=1).astype(jnp.float32)


def tile_numbers(key):
    key = jax.random.fold_in(key, 102)
    keys = jax.random.split(key, 2)
    window = N_TILE * TILES_DEV
    starts = jax.random.randint(keys[0], (N_VIEW,), 0, 32400 - window + 1)
    starts = starts.at[0].set(0).at[N_VIEW - 1].set(32400 - window)
    order_key = jax.random.randint(keys[1], (N_VIEW, window), 0, 2 ** 30)
    order = jnp.argsort(order_key, axis=1, stable=True).astype(jnp.int32)
    numbers = starts[:, None] + order
    return numbers.reshape(N_VIEW, N_TILE, TILES_DEV).astype(jnp.int32)


def layout(key):
    key = jax.random.fold_in(key, 103)
    n_dev = N_TILE * N_VIEW
    cap_dev = G_DEV // n_dev
    keys = jax.random.split(key, 7)
    level = jax.random.randint(keys[0], (n_dev,), 0, 3)
    low = jnp.array([K // 2, K // 4, K // 8], jnp.int32)[level]
    high = jnp.array([K, K // 2, K // 4], jnp.int32)[level]
    length = low[:, None] + jax.random.randint(keys[1], (n_dev, TILES_DEV), 0, 2 ** 30) % (high - low + 1)[:, None]
    chosen_dev = jax.random.randint(keys[2], (), 0, n_dev)
    length = length.at[chosen_dev, 0].set(K).at[chosen_dev, 1].set(K // 8).astype(jnp.int32)
    used = jnp.sum(length, axis=1)
    token_key = jax.random.randint(keys[3], (n_dev, G_DEV), 0, 2 ** 30)
    full_src = jax.random.randint(keys[4], (n_dev,), 0, n_dev)
    src_of = jnp.arange(G_DEV, dtype=jnp.int32) % n_dev
    layer_of = jnp.arange(G_DEV, dtype=jnp.int32) // n_dev
    token_key = jnp.where(src_of[None, :] == full_src[:, None], -1, token_key)
    token_order = jnp.argsort(token_key, axis=1, stable=True)
    token_rank = jnp.argsort(token_order, axis=1, stable=True)
    chosen = (token_rank < used[:, None]).astype(jnp.int32)
    counts = jnp.sum(chosen.reshape(n_dev, cap_dev, n_dev), axis=1)
    live = layer_of[None, :] < counts[:, src_of]
    order_key = jax.random.randint(keys[5], (n_dev, G_DEV), 0, 2 ** 30)
    order_key = jnp.where(live, order_key, 2 ** 30)
    slot_order = jnp.argsort(order_key, axis=1, stable=True).astype(jnp.int32)
    offset = jnp.cumsum(length, axis=1) - length
    spots = offset[:, :, None] + jnp.arange(K, dtype=jnp.int32)[None, None, :] % length[:, :, None]
    lists = jnp.take_along_axis(slot_order, spots.reshape(n_dev, -1), axis=1).reshape(n_dev, TILES_DEV, K)
    slot_rank = jnp.argsort(slot_order, axis=1, stable=True).astype(jnp.int32)
    tile_of = jnp.sum((slot_rank[:, :, None] >= offset[:, None, :]).astype(jnp.int32), axis=2) - 1
    pos_of = slot_rank - jnp.take_along_axis(offset, tile_of, axis=1)
    perm_key = jax.random.randint(keys[6], (n_dev, G_DEV), 0, 2 ** 30)
    perm = jnp.argsort(perm_key, axis=1, stable=True).astype(jnp.int32)
    live_src = live.reshape(n_dev, cap_dev, n_dev).transpose(2, 1, 0)
    sends = jnp.where(live_src, perm.reshape(n_dev, cap_dev, n_dev), -1).astype(jnp.int32)
    return (lists.astype(jnp.int32), length, sends, live, tile_of, pos_of, perm)


def draw_camera(key, part):
    return camera_rows(key)


def draw_tile_ids(key, part):
    return tile_numbers(key)


def draw_send_index(key, part):
    sends = layout(key)[2]
    n_dev = N_TILE * N_VIEW
    return sends.reshape(n_dev, G_DEV // n_dev, N_TILE, N_VIEW)


def draw_tile_lists(key, part):
    lists = layout(key)[0]
    return lists.reshape(N_TILE, N_VIEW, TILES_DEV, K).transpose(1, 0, 2, 3)


def draw_tile_lengths(key, part):
    length = layout(key)[1]
    return length.reshape(N_TILE, N_VIEW, TILES_DEV).transpose(1, 0, 2)


def draw_gaussians(key, part):
    lists, length, sends, live, tile_of, pos_of, perm = layout(key)
    cameras = camera_rows(key)
    numbers = tile_numbers(key)
    key = jax.random.fold_in(key, 7)
    n_dev = N_TILE * N_VIEW
    shape = (n_dev, G_DEV)
    keys = jax.random.split(key, 10)
    inverse = jnp.argsort(perm, axis=1, stable=True).astype(jnp.int32)
    layer_of = inverse // n_dev
    target = inverse % n_dev
    source = jnp.arange(n_dev, dtype=jnp.int32)[:, None]
    slot = layer_of * n_dev + source
    sent = live[target, slot]
    tile_slot = jnp.clip(tile_of[target, slot], 0, TILES_DEV - 1)
    pos_slot = jnp.clip(pos_of[target, slot], 0, K - 1)
    view_of = target % N_VIEW
    row_of = target // N_VIEW
    number = numbers[view_of, row_of, tile_slot]
    jitter = jax.random.uniform(keys[0], shape, jnp.float32, 0.0, 1.0)
    depth = jnp.where(sent, 2.0 + 6.0 * (pos_slot.astype(jnp.float32) + jitter) / K, 2.0 + 6.0 * jitter)
    place_x = (number % 240 * 16).astype(jnp.float32) + jax.random.uniform(keys[1], shape, jnp.float32, -4.0, 20.0)
    place_y = (number // 240 * 16).astype(jnp.float32) + jax.random.uniform(keys[2], shape, jnp.float32, -4.0, 20.0)
    view_x = (place_x - 1920.0) / 2400.0 * depth - cameras[view_of, 9]
    view_y = (place_y - 1080.0) / 2400.0 * depth - cameras[view_of, 10]
    view_z = depth - cameras[view_of, 11]
    rows = [cameras[view_of, number_id] for number_id in range(9)]
    world_x = rows[0] * view_x + rows[3] * view_y + rows[6] * view_z
    world_y = rows[1] * view_x + rows[4] * view_y + rows[7] * view_z
    world_z = rows[2] * view_x + rows[5] * view_y + rows[8] * view_z
    sigma = jnp.exp(jax.random.uniform(keys[3], shape, jnp.float32, jnp.log(3.0), jnp.log(40.0)))
    spread = 0.3 * jax.random.normal(keys[4], (3,) + shape, jnp.float32)
    logit = jax.random.uniform(keys[5], shape, jnp.float32, -6.0, -2.0)
    colour_dc = jax.random.normal(keys[6], (3,) + shape, jnp.float32)
    colour_rest = 0.3 * jax.random.normal(keys[7], (45,) + shape, jnp.float32)
    log_scale = jnp.log(sigma * depth / 2400.0)[None] + spread
    quat_real = jax.random.uniform(keys[8], shape, jnp.float32, 0.5, 1.5)
    quat_rest = jax.random.uniform(keys[9], (3,) + shape, jnp.float32, -1.0, 1.0)
    coeffs = jnp.concatenate([colour_dc, colour_rest], axis=0)
    stacked = jnp.concatenate([world_x[None], world_y[None], world_z[None], log_scale, quat_real[None], quat_rest, logit[None], coeffs], axis=0)
    return stacked.reshape(59, n_dev * G_DEV).astype(jnp.float32)


def block_scale(own_key, shape, cuts, low, top_value):
    gain, own = 1.0, jax.random.fold_in(own_key, 6)
    for position, parts in cuts:
        heights = jnp.exp(jax.random.uniform(jax.random.fold_in(own, position), (parts,), jnp.float32, low / len(cuts), top_value / len(cuts)))
        gain = gain * jnp.repeat(heights, shape[position] // parts).reshape([-1 if axis == position else 1 for axis in range(len(shape))])
    return gain


def scatter_about(key, extent, deviation, most, cuts=(), kind=jnp.bfloat16):
    values = jax.random.normal(key, extent, jnp.float32) * deviation
    if len(cuts) > 0:
        values = block_scale(key, extent, cuts, -0.22, 0.18) * values
    return jnp.clip(values, min=-most, max=most).astype(kind)


def setup_inputs(seed: int = 0) -> dict:
    splits = jax.random.split(jax.random.key(seed), 8)
    gaussians = draw_gaussians(jax.random.fold_in(splits[7], 71), 0)
    camera = draw_camera(jax.random.fold_in(splits[7], 71), 0)
    send_index = draw_send_index(jax.random.fold_in(splits[7], 71), 0)
    tile_ids = draw_tile_ids(jax.random.fold_in(splits[7], 71), 0)
    tile_lists = draw_tile_lists(jax.random.fold_in(splits[7], 71), 0)
    tile_lengths = draw_tile_lengths(jax.random.fold_in(splits[7], 71), 0)
    pixel_grad = scatter_about(splits[6], (3, VIEWS, PIX), 1.0, 6.0, ((1, 4), (2, 128)), jnp.float32)
    return dict(gaussians=gaussians, camera=camera, send_index=send_index, tile_ids=tile_ids, tile_lists=tile_lists, tile_lengths=tile_lengths, pixel_grad=pixel_grad)


def project(params, camera_cols):
    focal = 2400.0
    rotation = [camera_cols[number] for number in range(9)]
    shift_x = camera_cols[9]
    shift_y = camera_cols[10]
    shift_z = camera_cols[11]
    world_x = params[0]
    world_y = params[1]
    world_z = params[2]
    view_x = rotation[0] * world_x + rotation[1] * world_y + rotation[2] * world_z + shift_x
    view_y = rotation[3] * world_x + rotation[4] * world_y + rotation[5] * world_z + shift_y
    depth = rotation[6] * world_x + rotation[7] * world_y + rotation[8] * world_z + shift_z
    scales = [jnp.exp(params[3 + number]) for number in range(3)]
    quat_real = params[6]
    quat_i = params[7]
    quat_j = params[8]
    quat_k = params[9]
    quat_norm = jnp.sqrt(quat_real * quat_real + quat_i * quat_i + quat_j * quat_j + quat_k * quat_k)
    quat_real = quat_real / quat_norm
    quat_i = quat_i / quat_norm
    quat_j = quat_j / quat_norm
    quat_k = quat_k / quat_norm
    spin = [[1.0 - 2.0 * (quat_j * quat_j + quat_k * quat_k), 2.0 * (quat_i * quat_j - quat_real * quat_k), 2.0 * (quat_i * quat_k + quat_real * quat_j)], [2.0 * (quat_i * quat_j + quat_real * quat_k), 1.0 - 2.0 * (quat_i * quat_i + quat_k * quat_k), 2.0 * (quat_j * quat_k - quat_real * quat_i)], [2.0 * (quat_i * quat_k - quat_real * quat_j), 2.0 * (quat_j * quat_k + quat_real * quat_i), 1.0 - 2.0 * (quat_i * quat_i + quat_j * quat_j)]]
    shaped = [[spin[row_id][col_id] * scales[col_id] for col_id in range(3)] for row_id in range(3)]
    inv_depth = focal / depth
    slope_x = focal * view_x / (depth * depth)
    slope_y = focal * view_y / (depth * depth)
    jac_top = [inv_depth * rotation[col_id] - slope_x * rotation[6 + col_id] for col_id in range(3)]
    jac_low = [inv_depth * rotation[3 + col_id] - slope_y * rotation[6 + col_id] for col_id in range(3)]
    proj_top = [jac_top[0] * shaped[0][col_id] + jac_top[1] * shaped[1][col_id] + jac_top[2] * shaped[2][col_id] for col_id in range(3)]
    proj_low = [jac_low[0] * shaped[0][col_id] + jac_low[1] * shaped[1][col_id] + jac_low[2] * shaped[2][col_id] for col_id in range(3)]
    cov_xx = proj_top[0] * proj_top[0] + proj_top[1] * proj_top[1] + proj_top[2] * proj_top[2] + 0.3
    cov_xy = proj_top[0] * proj_low[0] + proj_top[1] * proj_low[1] + proj_top[2] * proj_low[2]
    cov_yy = proj_low[0] * proj_low[0] + proj_low[1] * proj_low[1] + proj_low[2] * proj_low[2] + 0.3
    determ = cov_xx * cov_yy - cov_xy * cov_xy
    conic_a = cov_yy / determ
    conic_b = -cov_xy / determ
    conic_c = cov_xx / determ
    screen_x = focal * view_x / depth + 1920.0
    screen_y = focal * view_y / depth + 1080.0
    centre_x = -(rotation[0] * shift_x + rotation[3] * shift_y + rotation[6] * shift_z)
    centre_y = -(rotation[1] * shift_x + rotation[4] * shift_y + rotation[7] * shift_z)
    centre_z = -(rotation[2] * shift_x + rotation[5] * shift_y + rotation[8] * shift_z)
    ray_x = world_x - centre_x
    ray_y = world_y - centre_y
    ray_z = world_z - centre_z
    ray_len = jnp.sqrt(ray_x * ray_x + ray_y * ray_y + ray_z * ray_z)
    ray_x = ray_x / ray_len
    ray_y = ray_y / ray_len
    ray_z = ray_z / ray_len
    sq_x = ray_x * ray_x
    sq_y = ray_y * ray_y
    sq_z = ray_z * ray_z
    basis = [jnp.full_like(ray_x, 0.28209479177387814), -0.4886025119029199 * ray_y, 0.4886025119029199 * ray_z, -0.4886025119029199 * ray_x, 1.0925484305920792 * ray_x * ray_y, -1.0925484305920792 * ray_y * ray_z, 0.31539156525252005 * (2.0 * sq_z - sq_x - sq_y), -1.0925484305920792 * ray_x * ray_z, 0.5462742152960396 * (sq_x - sq_y), -0.5900435899266435 * ray_y * (3.0 * sq_x - sq_y), 2.890611442640554 * ray_x * ray_y * ray_z, -0.4570457994644658 * ray_y * (4.0 * sq_z - sq_x - sq_y), 0.3731763325901154 * ray_z * (2.0 * sq_z - 3.0 * sq_x - 3.0 * sq_y), -0.4570457994644658 * ray_x * (4.0 * sq_z - sq_x - sq_y), 1.445305721320277 * ray_z * (sq_x - sq_y), -0.5900435899266435 * ray_x * (sq_x - 3.0 * sq_y)]
    colours = []
    for channel in range(3):
        total = 0.5 + basis[0] * params[11 + channel]
        for degree in range(1, 16):
            total = total + basis[degree] * params[11 + 3 * degree + channel]
        colours.append(jnp.maximum(total, 0.0))
    opacity = jax.nn.sigmoid(params[10])
    return jnp.stack([screen_x, screen_y, conic_a, conic_b, conic_c, colours[0], colours[1], colours[2], opacity])

def pixel_grid(numbers):
    pixel = jnp.arange(256, dtype=jnp.int32)
    grid_x = (numbers % 240 * 16)[:, None] + (pixel % 16)[None, :]
    grid_y = (numbers // 240 * 16)[:, None] + (pixel // 16)[None, :]
    return (grid_x.astype(jnp.float32), grid_y.astype(jnp.float32))

def composite(gathered, live, grid_x, grid_y):
    delta_x = grid_x[:, :, None] - gathered[0][:, None, :]
    delta_y = grid_y[:, :, None] - gathered[1][:, None, :]
    power = -0.5 * (gathered[2][:, None, :] * delta_x * delta_x + gathered[4][:, None, :] * delta_y * delta_y) - gathered[3][:, None, :] * delta_x * delta_y
    alpha = (gathered[8] * live)[:, None, :] * jnp.exp(power)
    log_keep = jnp.log1p(-alpha)
    running = jnp.cumsum(log_keep, axis=-1)
    before = jnp.concatenate([jnp.zeros_like(running[..., :1]), running[..., :-1]], axis=-1)
    weight = jnp.exp(before) * alpha
    return jnp.einsum('bpk,cbk->cbp', weight, gathered[5:8], precision=lax.Precision.HIGHEST)

def reference(gaussians, camera, send_index, tile_ids, tile_lists, tile_lengths, pixel_grad):
    ranks = N_TILE * N_VIEW
    tiles = tile_lists.shape[2]
    length_k = tile_lists.shape[3]
    per_dev = gaussians.shape[1] // ranks
    cap_dev = send_index.shape[1]
    flat_send = send_index.reshape(ranks, cap_dev, ranks)
    flat_lists = tile_lists.reshape(N_VIEW * N_TILE, tiles, length_k)
    flat_lengths = tile_lengths.reshape(N_VIEW * N_TILE, tiles)
    flat_ids = tile_ids.reshape(N_VIEW * N_TILE, tiles)
    flat_grad = pixel_grad.reshape(3, N_VIEW * N_TILE, tiles * 256)
    sources = jnp.arange(ranks, dtype=jnp.int32)
    positions = jnp.arange(length_k, dtype=jnp.int32)

    def step(carry, device):
        tile_pos = device // N_VIEW
        view_pos = device % N_VIEW
        entry = view_pos * N_TILE + tile_pos
        targets = jnp.take(flat_send, device, axis=2).T
        sending = (targets >= 0).reshape(-1)
        columns = (sources[None, :] * per_dev + jnp.maximum(targets, 0)).reshape(-1).astype(jnp.int32)
        raw = jnp.take(gaussians, columns, axis=1)
        cam_cols = jnp.take(camera, view_pos, axis=0)[:, None]
        lists = jnp.take(flat_lists, entry, axis=0)
        lengths = jnp.take(flat_lengths, entry, axis=0)
        numbers = jnp.take(flat_ids, entry, axis=0)
        cotangent = jnp.take(flat_grad, entry, axis=1).reshape(3, tiles, 256)
        live = (positions[None, :] < lengths[:, None]).astype(jnp.float32)
        grid_x, grid_y = pixel_grid(numbers)

        def forward(params):
            splats = project(params, cam_cols)
            gathered = jnp.take(splats, lists, axis=1)
            return composite(gathered, live, grid_x, grid_y)
        picture, pull_back = jax.vjp(forward, raw)
        slot_grad = pull_back(cotangent)[0]
        slot_grad = jnp.where(sending[None, :], slot_grad, jnp.float32(0.0))
        carry = carry.at[:, columns].add(slot_grad)
        return (carry, picture)
    start = jnp.zeros(gaussians.shape, jnp.float32)
    grads, pictures = lax.scan(step, start, jnp.arange(ranks, dtype=jnp.int32))
    image = pictures.reshape(N_TILE, N_VIEW, 3, tiles * 256).transpose(2, 1, 0, 3).reshape(3, N_VIEW, N_TILE * tiles * 256)
    return (image, grads)
```

```python
import jax
import jax.numpy as jnp
from jax import lax
from jax.experimental import pallas as pl
from jax.experimental.pallas import tpu as pltpu
from jax.sharding import PartitionSpec as P

F32 = jnp.float32
BF16 = jnp.bfloat16
I32 = jnp.int32
MESH = pl.DeviceIdType.MESH
DEPTH = 16
PLANE = 32


def project(params, cam):
    focal = 2400.0
    rotation = cam[:9]
    shift_x, shift_y, shift_z = cam[9:]
    world_x, world_y, world_z = params[0:3]
    view_x = rotation[0] * world_x + rotation[1] * world_y + rotation[2] * world_z + shift_x
    view_y = rotation[3] * world_x + rotation[4] * world_y + rotation[5] * world_z + shift_y
    depth = rotation[6] * world_x + rotation[7] * world_y + rotation[8] * world_z + shift_z
    scales = [jnp.exp(params[3 + number]) for number in range(3)]
    quat_real, quat_i, quat_j, quat_k = params[6:10]
    quat_inv = 1.0 / jnp.sqrt(
        quat_real * quat_real + quat_i * quat_i + quat_j * quat_j + quat_k * quat_k
    )
    quat_real = quat_real * quat_inv
    quat_i = quat_i * quat_inv
    quat_j = quat_j * quat_inv
    quat_k = quat_k * quat_inv
    spin = [
        [
            1.0 - 2.0 * (quat_j * quat_j + quat_k * quat_k),
            2.0 * (quat_i * quat_j - quat_real * quat_k),
            2.0 * (quat_i * quat_k + quat_real * quat_j),
        ],
        [
            2.0 * (quat_i * quat_j + quat_real * quat_k),
            1.0 - 2.0 * (quat_i * quat_i + quat_k * quat_k),
            2.0 * (quat_j * quat_k - quat_real * quat_i),
        ],
        [
            2.0 * (quat_i * quat_k - quat_real * quat_j),
            2.0 * (quat_j * quat_k + quat_real * quat_i),
            1.0 - 2.0 * (quat_i * quat_i + quat_j * quat_j),
        ],
    ]
    shaped = [[spin[row][col] * scales[col] for col in range(3)] for row in range(3)]
    depth_inv = 1.0 / depth
    inv_depth = focal * depth_inv
    screen_x = inv_depth * view_x
    screen_y = inv_depth * view_y
    slope_x = screen_x * depth_inv
    slope_y = screen_y * depth_inv
    jac_top = [inv_depth * rotation[col] - slope_x * rotation[6 + col] for col in range(3)]
    jac_low = [inv_depth * rotation[3 + col] - slope_y * rotation[6 + col] for col in range(3)]
    proj_top = [
        jac_top[0] * shaped[0][col] + jac_top[1] * shaped[1][col] + jac_top[2] * shaped[2][col]
        for col in range(3)
    ]
    proj_low = [
        jac_low[0] * shaped[0][col] + jac_low[1] * shaped[1][col] + jac_low[2] * shaped[2][col]
        for col in range(3)
    ]
    cov_xx = proj_top[0] * proj_top[0] + proj_top[1] * proj_top[1] + proj_top[2] * proj_top[2] + 0.3
    cov_xy = proj_top[0] * proj_low[0] + proj_top[1] * proj_low[1] + proj_top[2] * proj_low[2]
    cov_yy = proj_low[0] * proj_low[0] + proj_low[1] * proj_low[1] + proj_low[2] * proj_low[2] + 0.3
    det_inv = 1.0 / (cov_xx * cov_yy - cov_xy * cov_xy)
    conic_a = cov_yy * det_inv
    conic_b = -cov_xy * det_inv
    conic_c = cov_xx * det_inv
    centre_x = -(rotation[0] * shift_x + rotation[3] * shift_y + rotation[6] * shift_z)
    centre_y = -(rotation[1] * shift_x + rotation[4] * shift_y + rotation[7] * shift_z)
    centre_z = -(rotation[2] * shift_x + rotation[5] * shift_y + rotation[8] * shift_z)
    ray_x = world_x - centre_x
    ray_y = world_y - centre_y
    ray_z = world_z - centre_z
    ray_inv = 1.0 / jnp.sqrt(ray_x * ray_x + ray_y * ray_y + ray_z * ray_z)
    ray_x = ray_x * ray_inv
    ray_y = ray_y * ray_inv
    ray_z = ray_z * ray_inv
    sq_x = ray_x * ray_x
    sq_y = ray_y * ray_y
    sq_z = ray_z * ray_z
    basis = [
        -0.4886025119029199 * ray_y,
        0.4886025119029199 * ray_z,
        -0.4886025119029199 * ray_x,
        1.0925484305920792 * ray_x * ray_y,
        -1.0925484305920792 * ray_y * ray_z,
        0.31539156525252005 * (2.0 * sq_z - sq_x - sq_y),
        -1.0925484305920792 * ray_x * ray_z,
        0.5462742152960396 * (sq_x - sq_y),
        -0.5900435899266435 * ray_y * (3.0 * sq_x - sq_y),
        2.890611442640554 * ray_x * ray_y * ray_z,
        -0.4570457994644658 * ray_y * (4.0 * sq_z - sq_x - sq_y),
        0.3731763325901154 * ray_z * (2.0 * sq_z - 3.0 * sq_x - 3.0 * sq_y),
        -0.4570457994644658 * ray_x * (4.0 * sq_z - sq_x - sq_y),
        1.445305721320277 * ray_z * (sq_x - sq_y),
        -0.5900435899266435 * ray_x * (sq_x - 3.0 * sq_y),
    ]
    colours = []
    for channel in range(3):
        total = 0.5 + 0.28209479177387814 * params[11 + channel]
        for degree in range(1, 16):
            total = total + basis[degree - 1] * params[11 + 3 * degree + channel]
        colours.append(jnp.maximum(total, 0.0))
    return (screen_x + 1920.0, screen_y + 1080.0, conic_a, conic_b, conic_c, *colours)


def iotas(shape):
    return (lax.broadcasted_iota(I32, shape, 0), lax.broadcasted_iota(I32, shape, 1))


def take_lanes(values, lanes):
    return jnp.take_along_axis(
        jnp.broadcast_to(values, lanes.shape), lanes, axis=1, mode="promise_in_bounds"
    )


def lookup(tables, rows, lanes, start=None):
    results = [start] * len(tables)
    for row in range(tables[0].shape[0]):
        here = rows == row
        for number, table in enumerate(tables):
            taken = take_lanes(table[row : row + 1, :], lanes)
            if results[number] is None:
                results[number] = taken
            else:
                results[number] = jnp.where(here, taken, results[number])
    return results


def split2(values):
    high = values.astype(BF16).astype(F32)
    return (high, (values - high).astype(BF16).astype(F32))


def split3(values):
    high = values.astype(BF16).astype(F32)
    rest = values - high
    mid = rest.astype(BF16).astype(F32)
    return (high, mid, (rest - mid).astype(BF16).astype(F32))


def inverse(targets):
    count = targets.shape[0]
    target_row = targets >> 7
    target_lane = targets & 127
    sub8, _ = iotas((8, 128))
    sub128, _ = iotas((128, 128))
    lane = lax.broadcasted_iota(I32, (1, 128), 1).astype(F32)
    left, right = [], []
    for row in range(count):
        match = target_row[row : row + 1, :] == sub8
        low = jnp.where(match, lane, 0.0)
        high = jnp.where(match, float(row + 1), 0.0)
        left.append(jnp.concatenate([low, high], axis=0))
        right.append(jnp.where(target_lane[row : row + 1, :] == sub128, 1.0, 0.0))
    left = jnp.concatenate(left, axis=1).astype(BF16)
    right = jnp.concatenate(right, axis=1).astype(BF16)
    found = nt(left, right).astype(I32)
    return (found[8:16] - 1, found[0:8])


def nt(left, right):
    return lax.dot_general(
        left, right, (((1,), (1,)), ((), ())), preferred_element_type=F32
    )


def nn(left, right):
    return jnp.dot(left, right, preferred_element_type=F32)


def exchange(values, where_am_i, bufs):
    my_z, my_m, tile, view = where_am_i
    first_out, first_in, second_out, second_in, mixed, send1, recv1, send2, recv2 = bufs
    _, lane8 = iotas((8, 128))
    sub8, _ = iotas((8, 128))
    _, lane4 = iotas((4, 128))
    quarter8 = lane8 & 3
    for part in range(4):
        spot = part * 32 + (lane8 >> 2)
        for group in range(2):
            packed = take_lanes(values[4 * group], spot)
            for q in range(1, 4):
                packed = jnp.where(quarter8 == q, take_lanes(values[4 * group + q], spot), packed)
            for c in range(2):
                first_out[pl.ds(part * 8 + 2 * group + c, 4, stride=32), :] = packed[
                    4 * c : 4 * c + 4
                ]
        last = take_lanes(values[8], spot)
        first_out[pl.ds(part * 8 + 4, 4, stride=32), :] = jnp.where(
            (lane4 & 3) == 0, last[0:4], last[4:8]
        )

    def first_copy(step):
        to = lax.rem(my_z + step, DEPTH)
        return pltpu.make_async_remote_copy(
            src_ref=first_out.at[pl.ds(pl.multiple_of(to * 8, 8), 8)],
            dst_ref=first_in.at[pl.ds(pl.multiple_of(my_z * 8, 8), 8)],
            send_sem=send1.at[to],
            recv_sem=recv1.at[my_z],
            device_id=(to * 8 + lax.rem(tile, 8), view),
            device_id_type=MESH,
        )

    def first_arrival(step):
        origin = lax.rem(my_z + step, DEPTH)
        block = first_in.at[pl.ds(pl.multiple_of(origin * 8, 8), 8)]
        return pltpu.make_async_copy(block, block, recv1.at[origin])

    def second_copy(step):
        to = lax.rem(my_m + step, PLANE)
        return pltpu.make_async_remote_copy(
            src_ref=second_out.at[to],
            dst_ref=second_in.at[my_m],
            send_sem=send2.at[to],
            recv_sem=recv2.at[my_m],
            device_id=(my_z * 8 + to // 4, lax.rem(to, 4)),
            device_id_type=MESH,
        )

    def second_arrival(step):
        origin = lax.rem(my_m + step, PLANE)
        block = second_in.at[origin]
        return pltpu.make_async_copy(block, block, recv2.at[origin])

    def each(count, action):
        def body(step, carry):
            action(step)
            return carry

        lax.fori_loop(1, count, body, 0)

    each(DEPTH, lambda step: first_copy(step).start())
    own = pl.ds(pl.multiple_of(my_z * 8, 8), 8)
    first_in[own, :] = first_out[own, :]
    each(DEPTH, lambda step: first_arrival(step).wait())
    second_out[...] = first_in[...].T.reshape(PLANE, 4, 128)
    each(PLANE, lambda step: second_copy(step).start())
    second_in[my_m] = second_out[my_m]
    each(PLANE, lambda step: second_arrival(step).wait())
    mixed[...] = second_in[...].reshape(128, 128).T
    each(DEPTH, lambda step: first_copy(step).wait_send())
    each(PLANE, lambda step: second_copy(step).wait_send())

    part8 = lane8 >> 5
    base = (lane8 & 31) << 2
    results = []
    for group in range(2):
        blocks = [
            jnp.concatenate(
                [mixed[pl.ds(part * 8 + 2 * group + c, 4, stride=32), :] for c in range(2)], axis=0
            )
            for part in range(4)
        ]
        for q in range(4):
            value = take_lanes(blocks[0], base + q)
            for part in range(1, 4):
                value = jnp.where(part8 == part, take_lanes(blocks[part], base + q), value)
            results.append(value)
    spot = base + (sub8 >> 2)
    value = None
    for part in range(4):
        block = mixed[pl.ds(part * 8 + 4, 4, stride=32), :]
        taken = take_lanes(jnp.concatenate([block, block], axis=0), spot)
        value = taken if value is None else jnp.where(part8 == part, taken, value)
    results.append(value)
    return results


def render(
    table, ids_ref, list_ref, len_ref, cot_ref, image_ref,
    coef_s, colour_s, power_s, shade_s, alpha_s, keep_s, weight_h, weight_l, after_s, grad_h, grad_l, sum_s, tint_s,
):
    sub4, lane4 = iotas((4, 128))
    low = jnp.concatenate([list_ref[t : t + 1, 0:128] for t in (0, 0, 1, 1)], axis=0)
    high = jnp.concatenate([list_ref[t : t + 1, 128:256] for t in (0, 0, 1, 1)], axis=0)
    spot = 32 * (lane4 & 3) + (sub4 & 1) * 16 + (lane4 >> 3)
    slots = jnp.where((lane4 & 7) < 4, take_lanes(low, spot), take_lanes(high, spot))
    entry = 32 * (lane4 & 7) + (sub4 & 1) * 16 + (lane4 >> 3)
    live = entry < jnp.where(sub4 < 2, len_ref[0, 0, 0], len_ref[0, 0, 1])
    back_row, back_lane = inverse(jnp.where(live, slots, -1))

    pos_x, pos_y, con_a, con_b, con_c, red, green, blue, log_o = lookup(
        table, slots >> 7, slots & 127
    )
    first_x = (ids_ref[0, 0, 0] % 240 * 16).astype(F32) + 7.5
    first_y = (ids_ref[0, 0, 0] // 240 * 16).astype(F32) + 7.5
    other_x = (ids_ref[0, 0, 1] % 240 * 16).astype(F32) + 7.5
    other_y = (ids_ref[0, 0, 1] // 240 * 16).astype(F32) + 7.5
    pos_x = pos_x - jnp.where(sub4 < 2, first_x, other_x)
    pos_y = pos_y - jnp.where(sub4 < 2, first_y, other_y)
    slope_x = con_a * pos_x + con_b * pos_y
    slope_y = con_c * pos_y + con_b * pos_x
    level = log_o - 0.5 * (slope_x * pos_x + slope_y * pos_y)
    coefs = [-0.5 * con_a, -0.5 * con_c, -con_b, slope_x, slope_y]
    coefs = [jnp.where(live, value, 0.0) for value in coefs]
    coefs.append(jnp.where(live, level, -1.0e5))
    for number, value in enumerate(coefs):
        for part, piece in enumerate(split3(value)):
            coef_s[pl.ds(3 * number + part, 4, stride=32), :] = piece
    colour_s[...] = jnp.zeros_like(colour_s)
    for channel, value in enumerate((red, green, blue)):
        piece_h, piece_l = split2(value)
        for part in range(4):
            coef_s[pl.ds(18 + 4 * channel + part, 4, stride=32), :] = (piece_h, piece_l)[part // 2]
        for block in range(4):
            cols = slice((block % 2) * 128, (block % 2) * 128 + 128)
            at = block // 2 * 16 + channel
            colour_s[at : at + 1, cols] = piece_h[block : block + 1, :]
            colour_s[at + 8 : at + 9, cols] = piece_l[block : block + 1, :]
    for row in (30, 31):
        coef_s[pl.ds(row, 4, stride=32), :] = jnp.zeros((4, 128), F32)

    row32, pixel = iotas((32, 256))
    local_x = (pixel & 15).astype(F32) - 7.5
    local_y = (pixel >> 4).astype(F32) - 7.5
    terms = [
        local_x * local_x,
        local_y * local_y,
        local_x * local_y,
        local_x,
        local_y,
        jnp.ones_like(local_x),
    ]
    basis = jnp.zeros_like(local_x)
    moments = jnp.zeros_like(local_x)
    for number, term in enumerate(terms):
        basis = jnp.where((row32 >= 3 * number) & (row32 < 3 * number + 3), term, basis)
        moments = jnp.where(row32 == number, term, moments)
    basis = basis.astype(BF16)
    moments = moments[0:16].astype(BF16)
    cot_rows = []
    for t in range(2):
        shade = jnp.zeros_like(local_x)
        sums = jnp.zeros_like(local_x)
        for channel in range(3):
            value = cot_ref[channel, 0:1, t * 256 : t * 256 + 256]
            piece_h, piece_l = split2(value)
            start = 18 + 4 * channel
            shade = jnp.where((row32 == start) | (row32 == start + 2), piece_h, shade)
            shade = jnp.where((row32 == start + 1) | (row32 == start + 3), piece_l, shade)
            sums = jnp.where(row32 == channel, piece_h, sums)
            sums = jnp.where(row32 == channel + 8, piece_l, sums)
        cot_rows.append(sums[0:16].astype(BF16))
        left = jnp.concatenate(
            [coef_s[(2 * t + h) * 32 : (2 * t + h) * 32 + 32, :].T for h in range(2)], axis=0
        ).astype(BF16)
        power_s[t * 256 : t * 256 + 256, :] = nn(left, basis)
        shade_s[t * 256 : t * 256 + 256, :] = nn(left, shade.astype(BF16))

    def forward(step, kept):
        kept = list(kept)
        for t in range(2):
            for inner in range(4):
                rows = pl.ds(pl.multiple_of(t * 256 + step * 32 + inner * 8, 8), 8)
                alpha = jnp.exp(power_s[rows, :])
                alpha_s[rows, :] = alpha
                keep_s[rows, :] = kept[t]
                kept[t] = kept[t] * (1.0 - alpha)
        return tuple(kept)

    ones = jnp.ones((8, 256), F32)
    kept = lax.fori_loop(0, 8, forward, (ones, ones))
    sub_k, _ = iotas((8, 256))

    def ahead(values):
        result = jnp.where(sub_k >= 1, pltpu.roll(values, 1, 0), 1.0)
        for shift in (1, 2, 4):
            result = result * jnp.where(sub_k >= shift, pltpu.roll(result, shift, 0), 1.0)
        return result

    def behind(values):
        result = jnp.where(sub_k < 7, pltpu.roll(values, 7, 0), 0.0)
        for shift in (1, 2, 4):
            result = result + jnp.where(sub_k < 8 - shift, pltpu.roll(result, 8 - shift, 0), 0.0)
        return result

    entering = [ahead(kept[t]) for t in range(2)]

    def backward(step, sums):
        sums = list(sums)
        for t in range(2):
            for pair in (1, 0):
                start = t * 256 + (7 - step) * 32 + pair * 16
                weights = [None, None]
                for half in (1, 0):
                    rows = pl.ds(pl.multiple_of(start + half * 8, 8), 8)
                    weight = keep_s[rows, :] * entering[t] * alpha_s[rows, :]
                    gain = weight * shade_s[rows, :]
                    weights[half] = weight
                    after_s[rows, :] = sums[t]
                    power_s[rows, :] = gain
                    sums[t] = sums[t] + gain
                weight = jnp.concatenate(weights, axis=0)
                rows = pl.ds(pl.multiple_of(start, 16), 16)
                piece = weight.astype(BF16)
                weight_h[rows, :] = piece
                weight_l[rows, :] = (weight - piece.astype(F32)).astype(BF16)
        return tuple(sums)

    zeros = jnp.zeros((8, 256), F32)
    sums = lax.fori_loop(0, 8, backward, (zeros, zeros))
    leaving = [behind(sums[t]) for t in range(2)]
    leaving = [jnp.concatenate([value, value], axis=0) for value in leaving]

    def slopes(step, carry):
        for t in range(2):
            for pair in range(2):
                rows = pl.ds(pl.multiple_of(t * 256 + step * 32 + pair * 16, 16), 16)
                alpha = alpha_s[rows, :]
                ratio = alpha / (1.0 - alpha)
                grad = power_s[rows, :] - ratio * (after_s[rows, :] + leaving[t])
                piece = grad.astype(BF16)
                grad_h[rows, :] = piece
                grad_l[rows, :] = (grad - piece.astype(F32)).astype(BF16)
        return carry

    lax.fori_loop(0, 8, slopes, 0)

    for t in range(2):
        rows = slice(t * 256, t * 256 + 256)
        tints = colour_s[t * 16 : t * 16 + 16, :].astype(BF16)
        picture = nn(tints, weight_h[rows, :]) + nn(tints, weight_l[rows, :])
        picture = picture[0:8] + picture[8:16]
        for channel in range(3):
            image_ref[channel, 0:1, rows] = picture[channel : channel + 1, :]
        total = nt(moments, grad_h[rows, :]) + nt(moments, grad_l[rows, :])
        tint = nt(cot_rows[t], weight_h[rows, :]) + nt(cot_rows[t], weight_l[rows, :])
        tint = tint[0:8] + tint[8:16]
        for h in range(2):
            cols = slice(h * 128, h * 128 + 128)
            at = (2 * t + h) * 8
            sum_s[at : at + 8, :] = total[0:8, cols]
            tint_s[at : at + 8, :] = tint[:, cols]

    sum_xx, sum_yy, sum_xy, sum_x, sum_y, sum_1 = [
        sum_s[pl.ds(number, 4, stride=8), :] for number in range(6)
    ]
    tints = [tint_s[pl.ds(number, 4, stride=8), :] for number in range(3)]
    first_mx = sum_x - pos_x * sum_1
    first_my = sum_y - pos_y * sum_1
    grads = [
        con_a * first_mx + con_b * first_my,
        con_c * first_my + con_b * first_mx,
        -0.5 * (sum_xx - pos_x * (sum_x + first_mx)),
        -(sum_xy - pos_x * sum_y - pos_y * first_mx),
        -0.5 * (sum_yy - pos_y * (sum_y + first_my)),
        *tints,
        sum_1,
    ]
    return lookup(grads, back_row, back_lane, jnp.zeros((8, 128), F32))


def kernel(
    gauss_ref, cam_ref, send_ref, ids_ref, list_ref, len_ref, cot_ref, image_ref, out_ref,
    spread, *scratch,
):
    there, back, work = scratch[0:9], scratch[9:18], scratch[18:]
    tile = lax.axis_index("tile")
    view = lax.axis_index("view")
    my_z = tile // 8
    my_m = lax.rem(tile, 8) * 4 + view
    where_am_i = (my_z, my_m, tile, view)

    barrier = pltpu.get_barrier_semaphore()

    def greet_plane(step, carry):
        to = lax.rem(my_z + step, DEPTH)
        pl.semaphore_signal(
            barrier, inc=1, device_id=(to * 8 + lax.rem(tile, 8), view), device_id_type=MESH
        )
        return carry

    def greet_column(step, carry):
        to = lax.rem(my_m + step, PLANE)
        pl.semaphore_signal(
            barrier, inc=1, device_id=(my_z * 8 + to // 4, lax.rem(to, 4)), device_id_type=MESH
        )
        return carry

    lax.fori_loop(1, DEPTH, greet_plane, 0)
    lax.fori_loop(1, PLANE, greet_column, 0)

    sub8, lane8 = iotas((8, 128))
    spot = (sub8 & 3) * 32 + (lane8 >> 2)
    targets = None
    for number in range(4):
        row = jnp.where(sub8 < 4, send_ref[number : number + 1, :], send_ref[4 + number : 5 + number, :])
        taken = take_lanes(row, spot)
        targets = taken if targets is None else jnp.where((lane8 & 3) == number, taken, targets)
    slot_row, slot_lane = inverse(targets)
    sent = slot_row >= 0
    cam = []
    for number in range(12):
        value = jnp.full((8, 128), cam_ref[0, number], F32)
        for other in range(1, 4):
            value = jnp.where((slot_lane & 3) == other, cam_ref[other, number], value)
        cam.append(value)

    for block in range(8):
        spread[pl.ds(block, 59, stride=8), :] = gauss_ref[:, block * 128 : block * 128 + 128]

    def read_params():
        return [spread[8 * number : 8 * number + 8, :] for number in range(59)]

    params = read_params()
    splats = list(project(params, cam))
    logit = params[10]
    splats.append(jnp.minimum(logit, 0.0) - jnp.log1p(jnp.exp(-jnp.abs(logit))))
    chosen = jnp.maximum(targets, 0)
    outgoing = lookup(splats, chosen >> 7, chosen & 127)

    pl.semaphore_wait(barrier, DEPTH + PLANE - 2)
    arrived = exchange(outgoing, where_am_i, there)
    slot_grads = render(arrived, ids_ref, list_ref, len_ref, cot_ref, image_ref, *work)
    returned = exchange(slot_grads, where_am_i, back)

    grads = lookup(returned, slot_row, slot_lane, jnp.zeros((8, 128), F32))
    params = read_params()
    _, pull_back = jax.vjp(lambda values: project(values, cam), params)
    (param_grads,) = pull_back(tuple(grads[0:8]))
    for number, value in enumerate(param_grads):
        if number == 10:
            value = grads[8] / (1.0 + jnp.exp(params[10]))
        spread[8 * number : 8 * number + 8, :] = jnp.where(sent, value, 0.0)
    for block in range(8):
        out_ref[:, block * 128 : block * 128 + 128] = spread[pl.ds(block, 59, stride=8), :]


def exchange_scratch():
    return [
        pltpu.VMEM((128, 128), F32),
        pltpu.VMEM((128, 128), F32),
        pltpu.VMEM((PLANE, 4, 128), F32),
        pltpu.VMEM((PLANE, 4, 128), F32),
        pltpu.VMEM((128, 128), F32),
        pltpu.SemaphoreType.DMA((DEPTH,)),
        pltpu.SemaphoreType.DMA((DEPTH,)),
        pltpu.SemaphoreType.DMA((PLANE,)),
        pltpu.SemaphoreType.DMA((PLANE,)),
    ]


def render_scratch():
    return [
        pltpu.VMEM((128, 128), F32),
        pltpu.VMEM((32, 256), F32),
        pltpu.VMEM((512, 256), F32),
        pltpu.VMEM((512, 256), F32),
        pltpu.VMEM((512, 256), F32),
        pltpu.VMEM((512, 256), F32),
        pltpu.VMEM((512, 256), BF16),
        pltpu.VMEM((512, 256), BF16),
        pltpu.VMEM((512, 256), F32),
        pltpu.VMEM((512, 256), BF16),
        pltpu.VMEM((512, 256), BF16),
        pltpu.VMEM((32, 128), F32),
        pltpu.VMEM((32, 128), F32),
    ]


def per_device(gaussians, camera, send_index, tile_ids, tile_lists, tile_lengths, pixel_grad):
    sends = jnp.transpose(send_index, (0, 1, 3, 2)).reshape(8, 128)
    lists = tile_lists.reshape(2, 256)
    vmem = pl.BlockSpec(memory_space=pltpu.VMEM)
    smem = pl.BlockSpec(memory_space=pltpu.SMEM)
    image, grads = pl.pallas_call(
        kernel,
        out_shape=(
            jax.ShapeDtypeStruct((3, 1, 512), F32),
            jax.ShapeDtypeStruct((59, 1024), F32),
        ),
        in_specs=[vmem, smem, vmem, smem, vmem, smem, vmem],
        out_specs=(vmem, vmem),
        scratch_shapes=[
            pltpu.VMEM((480, 128), F32),
            *exchange_scratch(),
            *exchange_scratch(),
            *render_scratch(),
        ],
        compiler_params=pltpu.CompilerParams(
            collective_id=0, has_side_effects=True, vmem_limit_bytes=32 * 1024 * 1024
        ),
    )(gaussians, camera, sends, tile_ids, lists, tile_lengths, pixel_grad)
    return (image, grads)


def solution(mesh):
    return jax.shard_map(
        per_device,
        mesh=mesh,
        in_specs=(
            P(None, ("tile", "view")),
            P(),
            P(("tile", "view"), None, None, None),
            P("view", "tile", None),
            P("view", "tile", None, None),
            P("view", "tile", None),
            P(None, "view", "tile"),
        ),
        out_specs=(P(None, "view", "tile"), P(None, ("tile", "view"))),
        check_vma=False,
    )
```

```python
import jax
import jax.numpy as jnp
from jax import lax
from jax.experimental import pallas as pl
from jax.experimental.pallas import tpu as pltpu
from jax.sharding import PartitionSpec as P

F32 = jnp.float32
BF16 = jnp.bfloat16
I32 = jnp.int32
MESH = pl.DeviceIdType.MESH
DEPTH = 16
PLANE = 32


def ring(distance, size):
    return min(distance, size - distance)


Z_STEPS = sorted(range(1, DEPTH), key=lambda step: -ring(step, DEPTH))
M_STEPS = sorted(
    [(x, core, y) for x in range(4) for core in range(2) for y in range(4) if x + core + y > 0],
    key=lambda step: -2 * (ring(step[0], 4) + ring(step[2], 4)) - step[1],
)


def project(params, cam):
    focal = 2400.0
    rotation = cam[:9]
    shift_x, shift_y, shift_z = cam[9:]
    world_x, world_y, world_z = params[0:3]
    view_x = rotation[0] * world_x + rotation[1] * world_y + rotation[2] * world_z + shift_x
    view_y = rotation[3] * world_x + rotation[4] * world_y + rotation[5] * world_z + shift_y
    depth = rotation[6] * world_x + rotation[7] * world_y + rotation[8] * world_z + shift_z
    scales = [jnp.exp(params[3 + number]) for number in range(3)]
    quat_real, quat_i, quat_j, quat_k = params[6:10]
    quat_inv = 1.0 / jnp.sqrt(
        quat_real * quat_real + quat_i * quat_i + quat_j * quat_j + quat_k * quat_k
    )
    quat_real = quat_real * quat_inv
    quat_i = quat_i * quat_inv
    quat_j = quat_j * quat_inv
    quat_k = quat_k * quat_inv
    spin = [
        [
            1.0 - 2.0 * (quat_j * quat_j + quat_k * quat_k),
            2.0 * (quat_i * quat_j - quat_real * quat_k),
            2.0 * (quat_i * quat_k + quat_real * quat_j),
        ],
        [
            2.0 * (quat_i * quat_j + quat_real * quat_k),
            1.0 - 2.0 * (quat_i * quat_i + quat_k * quat_k),
            2.0 * (quat_j * quat_k - quat_real * quat_i),
        ],
        [
            2.0 * (quat_i * quat_k - quat_real * quat_j),
            2.0 * (quat_j * quat_k + quat_real * quat_i),
            1.0 - 2.0 * (quat_i * quat_i + quat_j * quat_j),
        ],
    ]
    shaped = [[spin[row][col] * scales[col] for col in range(3)] for row in range(3)]
    depth_inv = 1.0 / depth
    inv_depth = focal * depth_inv
    screen_x = inv_depth * view_x
    screen_y = inv_depth * view_y
    slope_x = screen_x * depth_inv
    slope_y = screen_y * depth_inv
    jac_top = [inv_depth * rotation[col] - slope_x * rotation[6 + col] for col in range(3)]
    jac_low = [inv_depth * rotation[3 + col] - slope_y * rotation[6 + col] for col in range(3)]
    proj_top = [
        jac_top[0] * shaped[0][col] + jac_top[1] * shaped[1][col] + jac_top[2] * shaped[2][col]
        for col in range(3)
    ]
    proj_low = [
        jac_low[0] * shaped[0][col] + jac_low[1] * shaped[1][col] + jac_low[2] * shaped[2][col]
        for col in range(3)
    ]
    cov_xx = proj_top[0] * proj_top[0] + proj_top[1] * proj_top[1] + proj_top[2] * proj_top[2] + 0.3
    cov_xy = proj_top[0] * proj_low[0] + proj_top[1] * proj_low[1] + proj_top[2] * proj_low[2]
    cov_yy = proj_low[0] * proj_low[0] + proj_low[1] * proj_low[1] + proj_low[2] * proj_low[2] + 0.3
    det_inv = 1.0 / (cov_xx * cov_yy - cov_xy * cov_xy)
    conic_a = cov_yy * det_inv
    conic_b = -cov_xy * det_inv
    conic_c = cov_xx * det_inv
    centre_x = -(rotation[0] * shift_x + rotation[3] * shift_y + rotation[6] * shift_z)
    centre_y = -(rotation[1] * shift_x + rotation[4] * shift_y + rotation[7] * shift_z)
    centre_z = -(rotation[2] * shift_x + rotation[5] * shift_y + rotation[8] * shift_z)
    ray_x = world_x - centre_x
    ray_y = world_y - centre_y
    ray_z = world_z - centre_z
    ray_inv = 1.0 / jnp.sqrt(ray_x * ray_x + ray_y * ray_y + ray_z * ray_z)
    ray_x = ray_x * ray_inv
    ray_y = ray_y * ray_inv
    ray_z = ray_z * ray_inv
    sq_x = ray_x * ray_x
    sq_y = ray_y * ray_y
    sq_z = ray_z * ray_z
    basis = [
        -0.4886025119029199 * ray_y,
        0.4886025119029199 * ray_z,
        -0.4886025119029199 * ray_x,
        1.0925484305920792 * ray_x * ray_y,
        -1.0925484305920792 * ray_y * ray_z,
        0.31539156525252005 * (2.0 * sq_z - sq_x - sq_y),
        -1.0925484305920792 * ray_x * ray_z,
        0.5462742152960396 * (sq_x - sq_y),
        -0.5900435899266435 * ray_y * (3.0 * sq_x - sq_y),
        2.890611442640554 * ray_x * ray_y * ray_z,
        -0.4570457994644658 * ray_y * (4.0 * sq_z - sq_x - sq_y),
        0.3731763325901154 * ray_z * (2.0 * sq_z - 3.0 * sq_x - 3.0 * sq_y),
        -0.4570457994644658 * ray_x * (4.0 * sq_z - sq_x - sq_y),
        1.445305721320277 * ray_z * (sq_x - sq_y),
        -0.5900435899266435 * ray_x * (sq_x - 3.0 * sq_y),
    ]
    colours = []
    for channel in range(3):
        total = 0.5 + 0.28209479177387814 * params[11 + channel]
        for degree in range(1, 16):
            total = total + basis[degree - 1] * params[11 + 3 * degree + channel]
        colours.append(jnp.maximum(total, 0.0))
    return (screen_x + 1920.0, screen_y + 1080.0, conic_a, conic_b, conic_c, *colours)


def iotas(shape):
    return (lax.broadcasted_iota(I32, shape, 0), lax.broadcasted_iota(I32, shape, 1))


def take_lanes(values, lanes):
    return jnp.take_along_axis(
        jnp.broadcast_to(values, lanes.shape), lanes, axis=1, mode="promise_in_bounds"
    )


def lookup(tables, rows, lanes, start=None):
    results = [start] * len(tables)
    for row in range(tables[0].shape[0]):
        here = rows == row
        for number, table in enumerate(tables):
            taken = take_lanes(table[row : row + 1, :], lanes)
            if results[number] is None:
                results[number] = taken
            else:
                results[number] = jnp.where(here, taken, results[number])
    return results


def split2(values):
    high = values.astype(BF16).astype(F32)
    return (high, (values - high).astype(BF16).astype(F32))


def split3(values):
    high = values.astype(BF16).astype(F32)
    rest = values - high
    mid = rest.astype(BF16).astype(F32)
    return (high, mid, (rest - mid).astype(BF16).astype(F32))


def inverse(targets):
    count = targets.shape[0]
    target_row = targets >> 7
    target_lane = targets & 127
    sub8, _ = iotas((8, 128))
    sub128, _ = iotas((128, 128))
    lane = lax.broadcasted_iota(I32, (1, 128), 1).astype(F32)
    left, right = [], []
    for row in range(count):
        match = target_row[row : row + 1, :] == sub8
        low = jnp.where(match, lane, 0.0)
        high = jnp.where(match, float(row + 1), 0.0)
        left.append(jnp.concatenate([low, high], axis=0))
        right.append(jnp.where(target_lane[row : row + 1, :] == sub128, 1.0, 0.0))
    left = jnp.concatenate(left, axis=1).astype(BF16)
    right = jnp.concatenate(right, axis=1).astype(BF16)
    found = nt(left, right).astype(I32)
    return (found[8:16] - 1, found[0:8])


def nt(left, right):
    return lax.dot_general(
        left, right, (((1,), (1,)), ((), ())), preferred_element_type=F32
    )


def nn(left, right):
    return jnp.dot(left, right, preferred_element_type=F32)


def exchange(values, where_am_i, bufs, meanwhile=lambda: None):
    my_z, my_m, z_partners, m_partners = where_am_i
    first_out, first_in, second_out, second_in, mixed, send1, recv1, send2, recv2 = bufs
    _, lane8 = iotas((8, 128))
    sub8, _ = iotas((8, 128))
    _, lane4 = iotas((4, 128))
    quarter8 = lane8 & 3
    for part in range(4):
        spot = part * 32 + (lane8 >> 2)
        for group in range(2):
            packed = take_lanes(values[4 * group], spot)
            for q in range(1, 4):
                packed = jnp.where(quarter8 == q, take_lanes(values[4 * group + q], spot), packed)
            for c in range(2):
                for plane in range(4):
                    row = 4 * c + plane
                    first_out[4 * plane + part, pl.ds(2 * group + c, 1)] = packed[row : row + 1]
        last = take_lanes(values[8], spot)
        last = jnp.where((lane4 & 3) == 0, last[0:4], last[4:8])
        for plane in range(4):
            first_out[4 * plane + part, pl.ds(4, 1)] = last[plane : plane + 1]

    for to, device in z_partners:
        copy = pltpu.make_async_remote_copy(
            src_ref=first_out.at[to, pl.ds(0, 5)],
            dst_ref=first_in.at[my_z, pl.ds(0, 5)],
            send_sem=send1,
            recv_sem=recv1,
            device_id=device,
            device_id_type=MESH,
        )
        copy.start()
    first_in[my_z] = first_out[my_z]
    extra = meanwhile()
    first_all = first_in.at[pl.ds(0, DEPTH - 1), pl.ds(0, 5)]
    pltpu.make_async_copy(first_all, first_all, recv1).wait()
    second_out[...] = first_in[...].reshape(128, 128).T.reshape(PLANE, 4, 128)
    for to, device in m_partners:
        copy = pltpu.make_async_remote_copy(
            src_ref=second_out.at[to],
            dst_ref=second_in.at[my_m],
            send_sem=send2,
            recv_sem=recv2,
            device_id=device,
            device_id_type=MESH,
        )
        copy.start()
    second_in[my_m] = second_out[my_m]
    pltpu.make_async_copy(first_all, first_all, send1).wait()
    second_all = second_in.at[pl.ds(0, PLANE - 1)]
    pltpu.make_async_copy(second_all, second_all, recv2).wait()
    mixed[...] = second_in[...].reshape(128, 128).T
    pltpu.make_async_copy(second_all, second_all, send2).wait()

    part8 = lane8 >> 5
    base = (lane8 & 31) << 2
    results = []
    for group in range(2):
        blocks = [
            jnp.concatenate(
                [mixed[pl.ds(part * 8 + 2 * group + c, 4, stride=32), :] for c in range(2)], axis=0
            )
            for part in range(4)
        ]
        for q in range(4):
            value = take_lanes(blocks[0], base + q)
            for part in range(1, 4):
                value = jnp.where(part8 == part, take_lanes(blocks[part], base + q), value)
            results.append(value)
    spot = base + (sub8 >> 2)
    value = None
    for part in range(4):
        block = mixed[pl.ds(part * 8 + 4, 4, stride=32), :]
        taken = take_lanes(jnp.concatenate([block, block], axis=0), spot)
        value = taken if value is None else jnp.where(part8 == part, taken, value)
    results.append(value)
    return results, extra


def prepare(ids_ref, list_ref, len_ref, cot_ref, colour_s, coef_s):
    sub4, lane4 = iotas((4, 128))
    low = jnp.concatenate([list_ref[t : t + 1, 0:128] for t in (0, 0, 1, 1)], axis=0)
    high = jnp.concatenate([list_ref[t : t + 1, 128:256] for t in (0, 0, 1, 1)], axis=0)
    spot = 32 * (lane4 & 3) + (sub4 & 1) * 16 + (lane4 >> 3)
    slots = jnp.where((lane4 & 7) < 4, take_lanes(low, spot), take_lanes(high, spot))
    entry = 32 * (lane4 & 7) + (sub4 & 1) * 16 + (lane4 >> 3)
    live = entry < jnp.where(sub4 < 2, len_ref[0, 0, 0], len_ref[0, 0, 1])
    back_row, back_lane = inverse(jnp.where(live, slots, -1))

    first_x = (ids_ref[0, 0, 0] % 240 * 16).astype(F32) + 7.5
    first_y = (ids_ref[0, 0, 0] // 240 * 16).astype(F32) + 7.5
    other_x = (ids_ref[0, 0, 1] % 240 * 16).astype(F32) + 7.5
    other_y = (ids_ref[0, 0, 1] // 240 * 16).astype(F32) + 7.5
    corner = (jnp.where(sub4 < 2, first_x, other_x), jnp.where(sub4 < 2, first_y, other_y))
    colour_s[...] = jnp.zeros_like(colour_s)
    for row in (30, 31):
        coef_s[pl.ds(row, 4, stride=32), :] = jnp.zeros((4, 128), F32)
    row32, pixel = iotas((32, 256))
    local_x = (pixel & 15).astype(F32) - 7.5
    local_y = (pixel >> 4).astype(F32) - 7.5
    terms = [
        local_x * local_x,
        local_y * local_y,
        local_x * local_y,
        local_x,
        local_y,
        jnp.ones_like(local_x),
    ]
    basis = jnp.zeros_like(local_x)
    moments = jnp.zeros_like(local_x)
    for number, term in enumerate(terms):
        basis = jnp.where((row32 >= 3 * number) & (row32 < 3 * number + 3), term, basis)
        moments = jnp.where(row32 == number, term, moments)
    basis = basis.astype(BF16)
    moments = moments[0:16].astype(BF16)
    cot_rows, shades = [], []
    for t in range(2):
        shade = jnp.zeros_like(local_x)
        sums = jnp.zeros_like(local_x)
        for channel in range(3):
            value = cot_ref[channel, 0:1, t * 256 : t * 256 + 256]
            piece_h, piece_l = split2(value)
            start = 18 + 4 * channel
            shade = jnp.where((row32 == start) | (row32 == start + 2), piece_h, shade)
            shade = jnp.where((row32 == start + 1) | (row32 == start + 3), piece_l, shade)
            sums = jnp.where(row32 == channel, piece_h, sums)
            sums = jnp.where(row32 == channel + 8, piece_l, sums)
        cot_rows.append(sums[0:16].astype(BF16))
        shades.append(shade.astype(BF16))
    return (live, slots >> 7, slots & 127, back_row, back_lane, corner, basis, moments, cot_rows, shades)


def render(
    table, prepared, image_ref,
    coef_s, colour_s, power_s, shade_s, alpha_s, keep_s, weight_h, weight_l, after_s, grad_h, grad_l, sum_s, tint_s,
):
    live, slot_row, slot_lane, back_row, back_lane, corner, basis, moments, cot_rows, shades = prepared
    pos_x, pos_y, con_a, con_b, con_c, red, green, blue, log_o = lookup(table, slot_row, slot_lane)
    pos_x = pos_x - corner[0]
    pos_y = pos_y - corner[1]
    slope_x = con_a * pos_x + con_b * pos_y
    slope_y = con_c * pos_y + con_b * pos_x
    level = log_o - 0.5 * (slope_x * pos_x + slope_y * pos_y)
    coefs = [-0.5 * con_a, -0.5 * con_c, -con_b, slope_x, slope_y]
    coefs = [jnp.where(live, value, 0.0) for value in coefs]
    coefs.append(jnp.where(live, level, -1.0e5))
    for number, value in enumerate(coefs):
        for part, piece in enumerate(split3(value)):
            coef_s[pl.ds(3 * number + part, 4, stride=32), :] = piece
    for channel, value in enumerate((red, green, blue)):
        piece_h, piece_l = split2(value)
        for part in range(4):
            coef_s[pl.ds(18 + 4 * channel + part, 4, stride=32), :] = (piece_h, piece_l)[part // 2]
        for block in range(4):
            cols = slice((block % 2) * 128, (block % 2) * 128 + 128)
            at = block // 2 * 16 + channel
            colour_s[at : at + 1, cols] = piece_h[block : block + 1, :]
            colour_s[at + 8 : at + 9, cols] = piece_l[block : block + 1, :]

    for t in range(2):
        left = jnp.concatenate(
            [coef_s[(2 * t + h) * 32 : (2 * t + h) * 32 + 32, :].T for h in range(2)], axis=0
        ).astype(BF16)
        power_s[t * 256 : t * 256 + 256, :] = nn(left, basis)
        shade_s[t * 256 : t * 256 + 256, :] = nn(left, shades[t])

    def forward(step, kept):
        kept = list(kept)
        for t in range(2):
            for inner in range(4):
                rows = pl.ds(pl.multiple_of(t * 256 + step * 32 + inner * 8, 8), 8)
                alpha = jnp.exp(power_s[rows, :])
                alpha_s[rows, :] = alpha
                keep_s[rows, :] = kept[t]
                kept[t] = kept[t] * (1.0 - alpha)
        return tuple(kept)

    ones = jnp.ones((8, 256), F32)
    kept = lax.fori_loop(0, 8, forward, (ones, ones))
    sub_k, _ = iotas((8, 256))

    def ahead(values):
        result = jnp.where(sub_k >= 1, pltpu.roll(values, 1, 0), 1.0)
        for shift in (1, 2, 4):
            result = result * jnp.where(sub_k >= shift, pltpu.roll(result, shift, 0), 1.0)
        return result

    def behind(values):
        result = jnp.where(sub_k < 7, pltpu.roll(values, 7, 0), 0.0)
        for shift in (1, 2, 4):
            result = result + jnp.where(sub_k < 8 - shift, pltpu.roll(result, 8 - shift, 0), 0.0)
        return result

    entering = [ahead(kept[t]) for t in range(2)]

    def backward(step, sums):
        sums = list(sums)
        for t in range(2):
            for pair in (1, 0):
                start = t * 256 + (7 - step) * 32 + pair * 16
                weights = [None, None]
                for half in (1, 0):
                    rows = pl.ds(pl.multiple_of(start + half * 8, 8), 8)
                    weight = keep_s[rows, :] * entering[t] * alpha_s[rows, :]
                    gain = weight * shade_s[rows, :]
                    weights[half] = weight
                    after_s[rows, :] = sums[t]
                    power_s[rows, :] = gain
                    sums[t] = sums[t] + gain
                weight = jnp.concatenate(weights, axis=0)
                rows = pl.ds(pl.multiple_of(start, 16), 16)
                piece = weight.astype(BF16)
                weight_h[rows, :] = piece
                weight_l[rows, :] = (weight - piece.astype(F32)).astype(BF16)
        return tuple(sums)

    zeros = jnp.zeros((8, 256), F32)
    sums = lax.fori_loop(0, 8, backward, (zeros, zeros))
    leaving = [behind(sums[t]) for t in range(2)]
    leaving = [jnp.concatenate([value, value], axis=0) for value in leaving]

    def slopes(step, carry):
        for t in range(2):
            for pair in range(2):
                rows = pl.ds(pl.multiple_of(t * 256 + step * 32 + pair * 16, 16), 16)
                alpha = alpha_s[rows, :]
                ratio = alpha / (1.0 - alpha)
                grad = power_s[rows, :] - ratio * (after_s[rows, :] + leaving[t])
                piece = grad.astype(BF16)
                grad_h[rows, :] = piece
                grad_l[rows, :] = (grad - piece.astype(F32)).astype(BF16)
        return carry

    lax.fori_loop(0, 8, slopes, 0)

    for t in range(2):
        rows = slice(t * 256, t * 256 + 256)
        tints = colour_s[t * 16 : t * 16 + 16, :].astype(BF16)
        picture = nn(tints, weight_h[rows, :]) + nn(tints, weight_l[rows, :])
        picture = picture[0:8] + picture[8:16]
        for channel in range(3):
            image_ref[channel, 0:1, rows] = picture[channel : channel + 1, :]
        total = nt(moments, grad_h[rows, :]) + nt(moments, grad_l[rows, :])
        tint = nt(cot_rows[t], weight_h[rows, :]) + nt(cot_rows[t], weight_l[rows, :])
        tint = tint[0:8] + tint[8:16]
        for h in range(2):
            cols = slice(h * 128, h * 128 + 128)
            at = (2 * t + h) * 8
            sum_s[at : at + 8, :] = total[0:8, cols]
            tint_s[at : at + 8, :] = tint[:, cols]

    sum_xx, sum_yy, sum_xy, sum_x, sum_y, sum_1 = [
        sum_s[pl.ds(number, 4, stride=8), :] for number in range(6)
    ]
    tints = [tint_s[pl.ds(number, 4, stride=8), :] for number in range(3)]
    first_mx = sum_x - pos_x * sum_1
    first_my = sum_y - pos_y * sum_1
    grads = [
        con_a * first_mx + con_b * first_my,
        con_c * first_my + con_b * first_mx,
        -0.5 * (sum_xx - pos_x * (sum_x + first_mx)),
        -(sum_xy - pos_x * sum_y - pos_y * first_mx),
        -0.5 * (sum_yy - pos_y * (sum_y + first_my)),
        *tints,
        sum_1,
    ]
    return lookup(grads, back_row, back_lane, jnp.zeros((8, 128), F32))


def kernel(
    gauss_hbm, cam_hbm, send_hbm, ids_hbm, list_hbm, len_hbm, cot_hbm, image_ref, out_ref,
    gauss_ref, cam_ref, send_ref, ids_ref, list_ref, len_ref, cot_ref, in_sem, spread, *scratch,
):
    there, back, work = scratch[0:9], scratch[9:18], scratch[18:]
    tile = lax.axis_index("tile")
    view = lax.axis_index("view")
    my_z = tile // 8
    mine = lax.rem(tile, 8)
    my_x, my_core = mine // 2, lax.rem(mine, 2)
    my_m = mine * 4 + view
    z_partners, m_partners = [], []
    for step in Z_STEPS:
        to = lax.rem(my_z + step, DEPTH)
        z_partners.append((to, (to * 8 + mine, view)))
    for x, core, y in M_STEPS:
        place = lax.rem(my_x + x, 4) * 2 + lax.rem(my_core + core, 2)
        row = lax.rem(view + y, 4)
        m_partners.append((place * 4 + row, (my_z * 8 + place, row)))
    where_am_i = (my_z, my_m, z_partners, m_partners)

    barrier = pltpu.get_barrier_semaphore()
    for _, device in z_partners + m_partners:
        pl.semaphore_signal(barrier, inc=1, device_id=device, device_id_type=MESH)

    inputs = [
        pltpu.make_async_copy(source, target, in_sem.at[number])
        for number, (source, target) in enumerate(
            [
                (send_hbm, send_ref),
                (gauss_hbm, gauss_ref),
                (cam_hbm, cam_ref),
                (ids_hbm, ids_ref),
                (list_hbm, list_ref),
                (len_hbm, len_ref),
                (cot_hbm, cot_ref),
            ]
        )
    ]
    for copy in inputs:
        copy.start()
    inputs[0].wait()

    sub8, lane8 = iotas((8, 128))
    spot = (sub8 & 3) * 32 + (lane8 >> 2)
    targets = None
    for number in range(4):
        row = jnp.where(sub8 < 4, send_ref[number : number + 1, :], send_ref[4 + number : 5 + number, :])
        taken = take_lanes(row, spot)
        targets = taken if targets is None else jnp.where((lane8 & 3) == number, taken, targets)
    slot_row, slot_lane = inverse(targets)
    sent = slot_row >= 0
    for copy in inputs[1:]:
        copy.wait()
    cam = []
    for number in range(12):
        value = jnp.full((8, 128), cam_ref[0, number], F32)
        for other in range(1, 4):
            value = jnp.where((slot_lane & 3) == other, cam_ref[other, number], value)
        cam.append(value)

    for block in range(8):
        spread[pl.ds(block, 59, stride=8), :] = gauss_ref[:, block * 128 : block * 128 + 128]

    def read_params():
        return [spread[8 * number : 8 * number + 8, :] for number in range(59)]

    params = read_params()
    splats, pull_back = jax.vjp(lambda values: project(values, cam), params)
    logit = params[10]
    splats = [*splats, jnp.minimum(logit, 0.0) - jnp.log1p(jnp.exp(-jnp.abs(logit)))]
    logit_slope = 1.0 / (1.0 + jnp.exp(logit))
    chosen = jnp.maximum(targets, 0)
    outgoing = lookup(splats, chosen >> 7, chosen & 127)

    pl.semaphore_wait(barrier, DEPTH + PLANE - 2)
    arrived, prepared = exchange(
        outgoing,
        where_am_i,
        there,
        lambda: prepare(ids_ref, list_ref, len_ref, cot_ref, work[1], work[0]),
    )
    slot_grads = render(arrived, prepared, image_ref, *work)
    returned, _ = exchange(slot_grads, where_am_i, back)

    grads = lookup(returned, slot_row, slot_lane, jnp.zeros((8, 128), F32))
    (param_grads,) = pull_back(tuple(grads[0:8]))
    for number, value in enumerate(param_grads):
        if number == 10:
            value = grads[8] * logit_slope
        spread[8 * number : 8 * number + 8, :] = jnp.where(sent, value, 0.0)
    for block in range(8):
        out_ref[:, block * 128 : block * 128 + 128] = spread[pl.ds(block, 59, stride=8), :]


def exchange_scratch():
    return [
        pltpu.VMEM((DEPTH, 8, 128), F32),
        pltpu.VMEM((DEPTH, 8, 128), F32),
        pltpu.VMEM((PLANE, 4, 128), F32),
        pltpu.VMEM((PLANE, 4, 128), F32),
        pltpu.VMEM((128, 128), F32),
        pltpu.SemaphoreType.DMA,
        pltpu.SemaphoreType.DMA,
        pltpu.SemaphoreType.DMA,
        pltpu.SemaphoreType.DMA,
    ]


def render_scratch():
    return [
        pltpu.VMEM((128, 128), F32),
        pltpu.VMEM((32, 256), F32),
        pltpu.VMEM((512, 256), F32),
        pltpu.VMEM((512, 256), F32),
        pltpu.VMEM((512, 256), F32),
        pltpu.VMEM((512, 256), F32),
        pltpu.VMEM((512, 256), BF16),
        pltpu.VMEM((512, 256), BF16),
        pltpu.VMEM((512, 256), F32),
        pltpu.VMEM((512, 256), BF16),
        pltpu.VMEM((512, 256), BF16),
        pltpu.VMEM((32, 128), F32),
        pltpu.VMEM((32, 128), F32),
    ]


def per_device(gaussians, camera, send_index, tile_ids, tile_lists, tile_lengths, pixel_grad):
    sends = jnp.transpose(send_index, (0, 1, 3, 2)).reshape(8, 128)
    lists = tile_lists.reshape(2, 256)
    vmem = pl.BlockSpec(memory_space=pltpu.VMEM)
    hbm = pl.BlockSpec(memory_space=pltpu.HBM)
    operands = [
        pltpu.with_memory_space_constraint(value, pltpu.HBM)
        for value in (gaussians, camera, sends, tile_ids, lists, tile_lengths, pixel_grad)
    ]
    image, grads = pl.pallas_call(
        kernel,
        out_shape=(
            jax.ShapeDtypeStruct((3, 1, 512), F32),
            jax.ShapeDtypeStruct((59, 1024), F32),
        ),
        in_specs=[hbm] * 7,
        out_specs=(vmem, vmem),
        scratch_shapes=[
            pltpu.VMEM((59, 1024), F32),
            pltpu.SMEM((4, 12), F32),
            pltpu.VMEM((8, 128), I32),
            pltpu.SMEM((1, 1, 2), I32),
            pltpu.VMEM((2, 256), I32),
            pltpu.SMEM((1, 1, 2), I32),
            pltpu.VMEM((3, 1, 512), F32),
            pltpu.SemaphoreType.DMA((7,)),
            pltpu.VMEM((480, 128), F32),
            *exchange_scratch(),
            *exchange_scratch(),
            *render_scratch(),
        ],
        compiler_params=pltpu.CompilerParams(
            collective_id=0, has_side_effects=True, vmem_limit_bytes=32 * 1024 * 1024
        ),
    )(*operands)
    return (image, grads)


def solution(mesh):
    return jax.shard_map(
        per_device,
        mesh=mesh,
        in_specs=(
            P(None, ("tile", "view")),
            P(),
            P(("tile", "view"), None, None, None),
            P("view", "tile", None),
            P("view", "tile", None, None),
            P("view", "tile", None),
            P(None, "view", "tile"),
        ),
        out_specs=(P(None, "view", "tile"), P(None, ("tile", "view"))),
        check_vma=False,
    )
```

```python
import jax
import jax.numpy as jnp
from jax import lax
from jax.experimental import pallas as pl
from jax.experimental.pallas import tpu as pltpu
from jax.sharding import PartitionSpec as P

F32 = jnp.float32
BF16 = jnp.bfloat16
I32 = jnp.int32
MESH = pl.DeviceIdType.MESH
DEPTH = 16
NEAR = 4
PLANE = 32


def ring(distance, size):
    return min(distance, size - distance)


Z_STEPS = sorted(range(1, DEPTH), key=lambda step: -ring(step, DEPTH))
M_STEPS = sorted(
    [(x, core, y) for x in range(4) for core in range(2) for y in range(4) if x + core + y > 0],
    key=lambda step: -2 * (ring(step[0], 4) + ring(step[2], 4)) - step[1],
)


def project(params, cam):
    focal = 2400.0
    rotation = cam[:9]
    shift_x, shift_y, shift_z = cam[9:]
    world_x, world_y, world_z = params[0:3]
    view_x = rotation[0] * world_x + rotation[1] * world_y + rotation[2] * world_z + shift_x
    view_y = rotation[3] * world_x + rotation[4] * world_y + rotation[5] * world_z + shift_y
    depth = rotation[6] * world_x + rotation[7] * world_y + rotation[8] * world_z + shift_z
    scales = [jnp.exp(params[3 + number]) for number in range(3)]
    quat_real, quat_i, quat_j, quat_k = params[6:10]
    quat_inv = 1.0 / jnp.sqrt(
        quat_real * quat_real + quat_i * quat_i + quat_j * quat_j + quat_k * quat_k
    )
    quat_real = quat_real * quat_inv
    quat_i = quat_i * quat_inv
    quat_j = quat_j * quat_inv
    quat_k = quat_k * quat_inv
    spin = [
        [
            1.0 - 2.0 * (quat_j * quat_j + quat_k * quat_k),
            2.0 * (quat_i * quat_j - quat_real * quat_k),
            2.0 * (quat_i * quat_k + quat_real * quat_j),
        ],
        [
            2.0 * (quat_i * quat_j + quat_real * quat_k),
            1.0 - 2.0 * (quat_i * quat_i + quat_k * quat_k),
            2.0 * (quat_j * quat_k - quat_real * quat_i),
        ],
        [
            2.0 * (quat_i * quat_k - quat_real * quat_j),
            2.0 * (quat_j * quat_k + quat_real * quat_i),
            1.0 - 2.0 * (quat_i * quat_i + quat_j * quat_j),
        ],
    ]
    shaped = [[spin[row][col] * scales[col] for col in range(3)] for row in range(3)]
    depth_inv = 1.0 / depth
    inv_depth = focal * depth_inv
    screen_x = inv_depth * view_x
    screen_y = inv_depth * view_y
    slope_x = screen_x * depth_inv
    slope_y = screen_y * depth_inv
    jac_top = [inv_depth * rotation[col] - slope_x * rotation[6 + col] for col in range(3)]
    jac_low = [inv_depth * rotation[3 + col] - slope_y * rotation[6 + col] for col in range(3)]
    proj_top = [
        jac_top[0] * shaped[0][col] + jac_top[1] * shaped[1][col] + jac_top[2] * shaped[2][col]
        for col in range(3)
    ]
    proj_low = [
        jac_low[0] * shaped[0][col] + jac_low[1] * shaped[1][col] + jac_low[2] * shaped[2][col]
        for col in range(3)
    ]
    cov_xx = proj_top[0] * proj_top[0] + proj_top[1] * proj_top[1] + proj_top[2] * proj_top[2] + 0.3
    cov_xy = proj_top[0] * proj_low[0] + proj_top[1] * proj_low[1] + proj_top[2] * proj_low[2]
    cov_yy = proj_low[0] * proj_low[0] + proj_low[1] * proj_low[1] + proj_low[2] * proj_low[2] + 0.3
    det_inv = 1.0 / (cov_xx * cov_yy - cov_xy * cov_xy)
    conic_a = cov_yy * det_inv
    conic_b = -cov_xy * det_inv
    conic_c = cov_xx * det_inv
    centre_x = -(rotation[0] * shift_x + rotation[3] * shift_y + rotation[6] * shift_z)
    centre_y = -(rotation[1] * shift_x + rotation[4] * shift_y + rotation[7] * shift_z)
    centre_z = -(rotation[2] * shift_x + rotation[5] * shift_y + rotation[8] * shift_z)
    ray_x = world_x - centre_x
    ray_y = world_y - centre_y
    ray_z = world_z - centre_z
    ray_inv = 1.0 / jnp.sqrt(ray_x * ray_x + ray_y * ray_y + ray_z * ray_z)
    ray_x = ray_x * ray_inv
    ray_y = ray_y * ray_inv
    ray_z = ray_z * ray_inv
    sq_x = ray_x * ray_x
    sq_y = ray_y * ray_y
    sq_z = ray_z * ray_z
    basis = [
        -0.4886025119029199 * ray_y,
        0.4886025119029199 * ray_z,
        -0.4886025119029199 * ray_x,
        1.0925484305920792 * ray_x * ray_y,
        -1.0925484305920792 * ray_y * ray_z,
        0.31539156525252005 * (2.0 * sq_z - sq_x - sq_y),
        -1.0925484305920792 * ray_x * ray_z,
        0.5462742152960396 * (sq_x - sq_y),
        -0.5900435899266435 * ray_y * (3.0 * sq_x - sq_y),
        2.890611442640554 * ray_x * ray_y * ray_z,
        -0.4570457994644658 * ray_y * (4.0 * sq_z - sq_x - sq_y),
        0.3731763325901154 * ray_z * (2.0 * sq_z - 3.0 * sq_x - 3.0 * sq_y),
        -0.4570457994644658 * ray_x * (4.0 * sq_z - sq_x - sq_y),
        1.445305721320277 * ray_z * (sq_x - sq_y),
        -0.5900435899266435 * ray_x * (sq_x - 3.0 * sq_y),
    ]
    colours = []
    for channel in range(3):
        total = 0.5 + 0.28209479177387814 * params[11 + channel]
        for degree in range(1, 16):
            total = total + basis[degree - 1] * params[11 + 3 * degree + channel]
        colours.append(jnp.maximum(total, 0.0))
    return (screen_x + 1920.0, screen_y + 1080.0, conic_a, conic_b, conic_c, *colours)


def iotas(shape):
    return (lax.broadcasted_iota(I32, shape, 0), lax.broadcasted_iota(I32, shape, 1))


def take_lanes(values, lanes):
    return jnp.take_along_axis(
        jnp.broadcast_to(values, lanes.shape), lanes, axis=1, mode="promise_in_bounds"
    )


def lookup(tables, rows, lanes, start=None):
    results = [start] * len(tables)
    for row in range(tables[0].shape[0]):
        here = rows == row
        for number, table in enumerate(tables):
            taken = take_lanes(table[row : row + 1, :], lanes)
            if results[number] is None:
                results[number] = taken
            else:
                results[number] = jnp.where(here, taken, results[number])
    return results


def split2(values):
    high = values.astype(BF16).astype(F32)
    return (high, (values - high).astype(BF16).astype(F32))


def split3(values):
    high = values.astype(BF16).astype(F32)
    rest = values - high
    mid = rest.astype(BF16).astype(F32)
    return (high, mid, (rest - mid).astype(BF16).astype(F32))


def inverse(targets):
    count = targets.shape[0]
    target_row = targets >> 7
    target_lane = targets & 127
    sub8, _ = iotas((8, 128))
    sub128, _ = iotas((128, 128))
    lane = lax.broadcasted_iota(I32, (1, 128), 1).astype(F32)
    left, right = [], []
    for row in range(count):
        match = target_row[row : row + 1, :] == sub8
        low = jnp.where(match, lane, 0.0)
        high = jnp.where(match, float(row + 1), 0.0)
        left.append(jnp.concatenate([low, high], axis=0))
        right.append(jnp.where(target_lane[row : row + 1, :] == sub128, 1.0, 0.0))
    left = jnp.concatenate(left, axis=1).astype(BF16)
    right = jnp.concatenate(right, axis=1).astype(BF16)
    found = nt(left, right).astype(I32)
    return (found[8:16] - 1, found[0:8])


def nt(left, right):
    return lax.dot_general(
        left, right, (((1,), (1,)), ((), ())), preferred_element_type=F32
    )


def nn(left, right):
    return jnp.dot(left, right, preferred_element_type=F32)


def exchange(values, where_am_i, bufs, meanwhile=lambda: None, between=lambda: None):
    my_z, my_m, z_partners, m_partners = where_am_i
    packs, plane_out, plane_in, depth_out, depth_in, send1, recv1, send2, recv2 = bufs
    _, lane8 = iotas((8, 128))
    sub8, _ = iotas((8, 128))
    _, lane4 = iotas((4, 128))
    quarter8 = lane8 & 3
    for part in range(4):
        spot = part * 32 + (lane8 >> 2)
        for group in range(2):
            packed = take_lanes(values[4 * group], spot)
            for q in range(1, 4):
                packed = jnp.where(quarter8 == q, take_lanes(values[4 * group + q], spot), packed)
            for c in range(2):
                for plane in range(4):
                    row = 4 * c + plane
                    packs[4 * plane + part, pl.ds(2 * group + c, 1)] = packed[row : row + 1]
        last = take_lanes(values[8], spot)
        last = jnp.where((lane4 & 3) == 0, last[0:4], last[4:8])
        for plane in range(4):
            packs[4 * plane + part, pl.ds(4, 1)] = last[plane : plane + 1]

    plane_out[...] = packs[...].reshape(128, 128).T.reshape(PLANE, 4, 128)
    for to, device in m_partners:
        pltpu.make_async_remote_copy(
            src_ref=plane_out.at[to],
            dst_ref=plane_in.at[my_m],
            send_sem=send1,
            recv_sem=recv1,
            device_id=device,
            device_id_type=MESH,
        ).start()
    plane_in[my_m] = plane_out[my_m]
    extra = meanwhile()
    plane_all = plane_in.at[pl.ds(0, PLANE - 1)]
    pltpu.make_async_copy(plane_all, plane_all, recv1).wait()
    depth_out[...] = plane_in[...].reshape(128, 128).T.reshape(DEPTH, 8, 128)
    between()
    for to, device in z_partners:
        pltpu.make_async_remote_copy(
            src_ref=depth_out.at[to, pl.ds(0, 5)],
            dst_ref=depth_in.at[pl.ds(pl.multiple_of(my_z * 8, 8), 5)],
            send_sem=send2,
            recv_sem=recv2,
            device_id=device,
            device_id_type=MESH,
        ).start()
    depth_in[pl.ds(pl.multiple_of(my_z * 8, 8), 8), :] = depth_out[my_z]
    pltpu.make_async_copy(plane_all, plane_all, send1).wait()
    depth_all = depth_out.at[pl.ds(0, DEPTH - 1), pl.ds(0, 5)]
    pltpu.make_async_copy(depth_all, depth_all, recv2).wait()
    pltpu.make_async_copy(depth_all, depth_all, send2).wait()

    part8 = lane8 >> 5
    base = (lane8 & 31) << 2
    results = []
    for group in range(2):
        blocks = [
            jnp.concatenate(
                [depth_in[pl.ds(part * 8 + 2 * group + c, 4, stride=32), :] for c in range(2)], axis=0
            )
            for part in range(4)
        ]
        for q in range(4):
            value = take_lanes(blocks[0], base + q)
            for part in range(1, 4):
                value = jnp.where(part8 == part, take_lanes(blocks[part], base + q), value)
            results.append(value)
    spot = base + (sub8 >> 2)
    value = None
    for part in range(4):
        block = depth_in[pl.ds(part * 8 + 4, 4, stride=32), :]
        taken = take_lanes(jnp.concatenate([block, block], axis=0), spot)
        value = taken if value is None else jnp.where(part8 == part, taken, value)
    results.append(value)
    return results, extra


def prepare(ids_ref, list_ref, len_ref, cot_ref, colour_s, coef_s):
    sub4, lane4 = iotas((4, 128))
    low = jnp.concatenate([list_ref[t : t + 1, 0:128] for t in (0, 0, 1, 1)], axis=0)
    high = jnp.concatenate([list_ref[t : t + 1, 128:256] for t in (0, 0, 1, 1)], axis=0)
    spot = 32 * (lane4 & 3) + (sub4 & 1) * 16 + (lane4 >> 3)
    slots = jnp.where((lane4 & 7) < 4, take_lanes(low, spot), take_lanes(high, spot))
    entry = 32 * (lane4 & 7) + (sub4 & 1) * 16 + (lane4 >> 3)
    live = entry < jnp.where(sub4 < 2, len_ref[0, 0, 0], len_ref[0, 0, 1])
    back_row, back_lane = inverse(jnp.where(live, slots, -1))

    first_x = (ids_ref[0, 0, 0] % 240 * 16).astype(F32) + 7.5
    first_y = (ids_ref[0, 0, 0] // 240 * 16).astype(F32) + 7.5
    other_x = (ids_ref[0, 0, 1] % 240 * 16).astype(F32) + 7.5
    other_y = (ids_ref[0, 0, 1] // 240 * 16).astype(F32) + 7.5
    corner = (jnp.where(sub4 < 2, first_x, other_x), jnp.where(sub4 < 2, first_y, other_y))
    colour_s[...] = jnp.zeros_like(colour_s)
    for row in (30, 31):
        coef_s[pl.ds(row, 4, stride=32), :] = jnp.zeros((4, 128), F32)
    row32, pixel = iotas((32, 256))
    local_x = (pixel & 15).astype(F32) - 7.5
    local_y = (pixel >> 4).astype(F32) - 7.5
    terms = [
        local_x * local_x,
        local_y * local_y,
        local_x * local_y,
        local_x,
        local_y,
        jnp.ones_like(local_x),
    ]
    basis = jnp.zeros_like(local_x)
    moments = jnp.zeros_like(local_x)
    for number, term in enumerate(terms):
        basis = jnp.where((row32 >= 3 * number) & (row32 < 3 * number + 3), term, basis)
        moments = jnp.where(row32 == number, term, moments)
    basis = basis.astype(BF16)
    moments = moments[0:16].astype(BF16)
    cot_rows, shades = [], []
    for t in range(2):
        shade = jnp.zeros_like(local_x)
        sums = jnp.zeros_like(local_x)
        for channel in range(3):
            value = cot_ref[channel, 0:1, t * 256 : t * 256 + 256]
            piece_h, piece_l = split2(value)
            start = 18 + 4 * channel
            shade = jnp.where((row32 == start) | (row32 == start + 2), piece_h, shade)
            shade = jnp.where((row32 == start + 1) | (row32 == start + 3), piece_l, shade)
            sums = jnp.where(row32 == channel, piece_h, sums)
            sums = jnp.where(row32 == channel + 8, piece_l, sums)
        cot_rows.append(sums[0:16].astype(BF16))
        shades.append(shade.astype(BF16))
    return (live, slots >> 7, slots & 127, back_row, back_lane, corner, basis, moments, cot_rows, shades)


def render(
    table, prepared, image_ref,
    coef_s, colour_s, power_s, shade_s, alpha_s, keep_s, weight_h, weight_l, after_s, grad_h, grad_l, sum_s, tint_s,
):
    live, slot_row, slot_lane, back_row, back_lane, corner, basis, moments, cot_rows, shades = prepared
    pos_x, pos_y, con_a, con_b, con_c, red, green, blue, log_o = lookup(table, slot_row, slot_lane)
    pos_x = pos_x - corner[0]
    pos_y = pos_y - corner[1]
    slope_x = con_a * pos_x + con_b * pos_y
    slope_y = con_c * pos_y + con_b * pos_x
    level = log_o - 0.5 * (slope_x * pos_x + slope_y * pos_y)
    coefs = [-0.5 * con_a, -0.5 * con_c, -con_b, slope_x, slope_y]
    coefs = [jnp.where(live, value, 0.0) for value in coefs]
    coefs.append(jnp.where(live, level, -1.0e5))
    for number, value in enumerate(coefs):
        for part, piece in enumerate(split3(value)):
            coef_s[pl.ds(3 * number + part, 4, stride=32), :] = piece
    for channel, value in enumerate((red, green, blue)):
        piece_h, piece_l = split2(value)
        for part in range(4):
            coef_s[pl.ds(18 + 4 * channel + part, 4, stride=32), :] = (piece_h, piece_l)[part // 2]
        for block in range(4):
            cols = slice((block % 2) * 128, (block % 2) * 128 + 128)
            at = block // 2 * 16 + channel
            colour_s[at : at + 1, cols] = piece_h[block : block + 1, :]
            colour_s[at + 8 : at + 9, cols] = piece_l[block : block + 1, :]

    for t in range(2):
        left = jnp.concatenate(
            [coef_s[(2 * t + h) * 32 : (2 * t + h) * 32 + 32, :].T for h in range(2)], axis=0
        ).astype(BF16)
        power_s[t * 256 : t * 256 + 256, :] = nn(left, basis)
        shade_s[t * 256 : t * 256 + 256, :] = nn(left, shades[t])

    def forward(step, kept):
        kept = list(kept)
        for t in range(2):
            for inner in range(4):
                rows = pl.ds(pl.multiple_of(t * 256 + step * 32 + inner * 8, 8), 8)
                alpha = jnp.exp(power_s[rows, :])
                alpha_s[rows, :] = alpha
                keep_s[rows, :] = kept[t]
                kept[t] = kept[t] * (1.0 - alpha)
        return tuple(kept)

    ones = jnp.ones((8, 256), F32)
    kept = (ones, ones)
    for step in range(8):
        kept = forward(step, kept)
    sub_k, _ = iotas((8, 256))

    def ahead(values):
        result = jnp.where(sub_k >= 1, pltpu.roll(values, 1, 0), 1.0)
        for shift in (1, 2, 4):
            result = result * jnp.where(sub_k >= shift, pltpu.roll(result, shift, 0), 1.0)
        return result

    def behind(values):
        result = jnp.where(sub_k < 7, pltpu.roll(values, 7, 0), 0.0)
        for shift in (1, 2, 4):
            result = result + jnp.where(sub_k < 8 - shift, pltpu.roll(result, 8 - shift, 0), 0.0)
        return result

    entering = [ahead(kept[t]) for t in range(2)]

    def backward(step, sums):
        sums = list(sums)
        for t in range(2):
            for pair in (1, 0):
                start = t * 256 + (7 - step) * 32 + pair * 16
                weights = [None, None]
                for half in (1, 0):
                    rows = pl.ds(pl.multiple_of(start + half * 8, 8), 8)
                    weight = keep_s[rows, :] * entering[t] * alpha_s[rows, :]
                    gain = weight * shade_s[rows, :]
                    weights[half] = weight
                    after_s[rows, :] = sums[t]
                    power_s[rows, :] = gain
                    sums[t] = sums[t] + gain
                weight = jnp.concatenate(weights, axis=0)
                rows = pl.ds(pl.multiple_of(start, 16), 16)
                piece = weight.astype(BF16)
                weight_h[rows, :] = piece
                weight_l[rows, :] = (weight - piece.astype(F32)).astype(BF16)
        return tuple(sums)

    zeros = jnp.zeros((8, 256), F32)
    sums = (zeros, zeros)
    for step in range(8):
        sums = backward(step, sums)
    leaving = [behind(sums[t]) for t in range(2)]
    leaving = [jnp.concatenate([value, value], axis=0) for value in leaving]

    def slopes(step, carry):
        for t in range(2):
            for pair in range(2):
                rows = pl.ds(pl.multiple_of(t * 256 + step * 32 + pair * 16, 16), 16)
                alpha = alpha_s[rows, :]
                ratio = alpha / (1.0 - alpha)
                grad = power_s[rows, :] - ratio * (after_s[rows, :] + leaving[t])
                piece = grad.astype(BF16)
                grad_h[rows, :] = piece
                grad_l[rows, :] = (grad - piece.astype(F32)).astype(BF16)
        return carry

    for step in range(8):
        slopes(step, 0)

    for t in range(2):
        rows = slice(t * 256, t * 256 + 256)
        tints = colour_s[t * 16 : t * 16 + 16, :].astype(BF16)
        picture = nn(tints, weight_h[rows, :]) + nn(tints, weight_l[rows, :])
        picture = picture[0:8] + picture[8:16]
        for channel in range(3):
            image_ref[channel, 0:1, rows] = picture[channel : channel + 1, :]
        total = nt(moments, grad_h[rows, :]) + nt(moments, grad_l[rows, :])
        tint = nt(cot_rows[t], weight_h[rows, :]) + nt(cot_rows[t], weight_l[rows, :])
        tint = tint[0:8] + tint[8:16]
        for h in range(2):
            cols = slice(h * 128, h * 128 + 128)
            at = (2 * t + h) * 8
            sum_s[at : at + 8, :] = total[0:8, cols]
            tint_s[at : at + 8, :] = tint[:, cols]

    sum_xx, sum_yy, sum_xy, sum_x, sum_y, sum_1 = [
        sum_s[pl.ds(number, 4, stride=8), :] for number in range(6)
    ]
    tints = [tint_s[pl.ds(number, 4, stride=8), :] for number in range(3)]
    first_mx = sum_x - pos_x * sum_1
    first_my = sum_y - pos_y * sum_1
    grads = [
        con_a * first_mx + con_b * first_my,
        con_c * first_my + con_b * first_mx,
        -0.5 * (sum_xx - pos_x * (sum_x + first_mx)),
        -(sum_xy - pos_x * sum_y - pos_y * first_mx),
        -0.5 * (sum_yy - pos_y * (sum_y + first_my)),
        *tints,
        sum_1,
    ]
    return lookup(grads, back_row, back_lane, jnp.zeros((8, 128), F32))


def kernel(
    gauss_hbm, cam_hbm, send_hbm, ids_hbm, list_hbm, len_hbm, cot_hbm, image_ref, out_ref,
    gauss_ref, cam_ref, send_ref, ids_ref, list_ref, len_ref, cot_ref, in_sem, far_sem, spread, *scratch,
):
    there, back, work = scratch[0:9], scratch[9:18], scratch[18:]
    tile = lax.axis_index("tile")
    view = lax.axis_index("view")
    my_z = tile // 8
    mine = lax.rem(tile, 8)
    my_x, my_core = mine // 2, lax.rem(mine, 2)
    my_m = mine * 4 + view
    z_partners, m_partners = [], []
    for step in Z_STEPS:
        to = lax.rem(my_z + step, DEPTH)
        z_partners.append((to, (to * 8 + mine, view)))
    for x, core, y in M_STEPS:
        place = lax.rem(my_x + x, 4) * 2 + lax.rem(my_core + core, 2)
        row = lax.rem(view + y, 4)
        m_partners.append((place * 4 + row, (my_z * 8 + place, row)))
    where_am_i = (my_z, my_m, z_partners, m_partners)

    barrier = pltpu.get_barrier_semaphore()
    near = [entry for step, entry in zip(Z_STEPS, z_partners) if ring(step, DEPTH) <= NEAR]
    for _, device in near + m_partners:
        pl.semaphore_signal(barrier, inc=1, device_id=device, device_id_type=MESH)

    inputs = [
        pltpu.make_async_copy(source, target, in_sem.at[number])
        for number, (source, target) in enumerate(
            [
                (send_hbm, send_ref),
                (gauss_hbm, gauss_ref),
                (cam_hbm, cam_ref),
                (ids_hbm, ids_ref),
                (list_hbm, list_ref),
                (len_hbm, len_ref),
                (cot_hbm, cot_ref),
            ]
        )
    ]
    for copy in inputs:
        copy.start()
    inputs[0].wait()

    sub8, lane8 = iotas((8, 128))
    spot = (sub8 & 3) * 32 + (lane8 >> 2)
    targets = None
    for number in range(4):
        row = jnp.where(sub8 < 4, send_ref[number : number + 1, :], send_ref[4 + number : 5 + number, :])
        taken = take_lanes(row, spot)
        targets = taken if targets is None else jnp.where((lane8 & 3) == number, taken, targets)
    slot_row, slot_lane = inverse(targets)
    sent = slot_row >= 0
    for copy in inputs[1:]:
        copy.wait()
    cam = []
    for number in range(12):
        value = jnp.full((8, 128), cam_ref[0, number], F32)
        for other in range(1, 4):
            value = jnp.where((slot_lane & 3) == other, cam_ref[other, number], value)
        cam.append(value)

    for block in range(8):
        spread[pl.ds(block, 59, stride=8), :] = gauss_ref[:, block * 128 : block * 128 + 128]

    def read_params():
        return [spread[8 * number : 8 * number + 8, :] for number in range(59)]

    params = read_params()
    splats, pull_back = jax.vjp(lambda values: project(values, cam), params)
    logit = params[10]
    splats = [*splats, jnp.minimum(logit, 0.0) - jnp.log1p(jnp.exp(-jnp.abs(logit)))]
    logit_slope = 1.0 / (1.0 + jnp.exp(logit))
    chosen = jnp.maximum(targets, 0)
    outgoing = lookup(splats, chosen >> 7, chosen & 127)

    pl.semaphore_wait(barrier, PLANE - 1 + 2 * NEAR)
    for step, (_, device) in zip(Z_STEPS, z_partners):
        if ring(step, DEPTH) == NEAR:
            pl.semaphore_signal(far_sem, inc=1, device_id=device, device_id_type=MESH)
    arrived, prepared = exchange(
        outgoing,
        where_am_i,
        there,
        lambda: prepare(ids_ref, list_ref, len_ref, cot_ref, work[1], work[0]),
        lambda: pl.semaphore_wait(far_sem, 2),
    )
    slot_grads = render(arrived, prepared, image_ref, *work)
    returned, _ = exchange(slot_grads, where_am_i, back)

    grads = lookup(returned, slot_row, slot_lane, jnp.zeros((8, 128), F32))
    (param_grads,) = pull_back(tuple(grads[0:8]))
    for number, value in enumerate(param_grads):
        if number == 10:
            value = grads[8] * logit_slope
        spread[8 * number : 8 * number + 8, :] = jnp.where(sent, value, 0.0)
    for block in range(8):
        out_ref[:, block * 128 : block * 128 + 128] = spread[pl.ds(block, 59, stride=8), :]


def exchange_scratch():
    return [
        pltpu.VMEM((DEPTH, 8, 128), F32),
        pltpu.VMEM((PLANE, 4, 128), F32),
        pltpu.VMEM((PLANE, 4, 128), F32),
        pltpu.VMEM((DEPTH, 8, 128), F32),
        pltpu.VMEM((128, 128), F32),
        pltpu.SemaphoreType.DMA,
        pltpu.SemaphoreType.DMA,
        pltpu.SemaphoreType.DMA,
        pltpu.SemaphoreType.DMA,
    ]


def render_scratch():
    return [
        pltpu.VMEM((128, 128), F32),
        pltpu.VMEM((32, 256), F32),
        pltpu.VMEM((512, 256), F32),
        pltpu.VMEM((512, 256), F32),
        pltpu.VMEM((512, 256), F32),
        pltpu.VMEM((512, 256), F32),
        pltpu.VMEM((512, 256), BF16),
        pltpu.VMEM((512, 256), BF16),
        pltpu.VMEM((512, 256), F32),
        pltpu.VMEM((512, 256), BF16),
        pltpu.VMEM((512, 256), BF16),
        pltpu.VMEM((32, 128), F32),
        pltpu.VMEM((32, 128), F32),
    ]


def per_device(gaussians, camera, send_index, tile_ids, tile_lists, tile_lengths, pixel_grad):
    sends = jnp.transpose(send_index, (0, 1, 3, 2)).reshape(8, 128)
    lists = tile_lists.reshape(2, 256)
    vmem = pl.BlockSpec(memory_space=pltpu.VMEM)
    hbm = pl.BlockSpec(memory_space=pltpu.HBM)
    operands = [
        pltpu.with_memory_space_constraint(value, pltpu.HBM)
        for value in (gaussians, camera, sends, tile_ids, lists, tile_lengths, pixel_grad)
    ]
    image, grads = pl.pallas_call(
        kernel,
        out_shape=(
            jax.ShapeDtypeStruct((3, 1, 512), F32),
            jax.ShapeDtypeStruct((59, 1024), F32),
        ),
        in_specs=[hbm] * 7,
        out_specs=(vmem, vmem),
        scratch_shapes=[
            pltpu.VMEM((59, 1024), F32),
            pltpu.SMEM((4, 12), F32),
            pltpu.VMEM((8, 128), I32),
            pltpu.SMEM((1, 1, 2), I32),
            pltpu.VMEM((2, 256), I32),
            pltpu.SMEM((1, 1, 2), I32),
            pltpu.VMEM((3, 1, 512), F32),
            pltpu.SemaphoreType.DMA((7,)),
            pltpu.SemaphoreType.REGULAR,
            pltpu.VMEM((480, 128), F32),
            *exchange_scratch(),
            *exchange_scratch(),
            *render_scratch(),
        ],
        compiler_params=pltpu.CompilerParams(
            collective_id=0, has_side_effects=True, vmem_limit_bytes=32 * 1024 * 1024
        ),
    )(*operands)
    return (image, grads)


def solution(mesh):
    return jax.shard_map(
        per_device,
        mesh=mesh,
        in_specs=(
            P(None, ("tile", "view")),
            P(),
            P(("tile", "view"), None, None, None),
            P("view", "tile", None),
            P("view", "tile", None, None),
            P("view", "tile", None),
            P(None, "view", "tile"),
        ),
        out_specs=(P(None, "view", "tile"), P(None, ("tile", "view"))),
        check_vma=False,
    )
```

```python
import jax
import jax.numpy as jnp
from jax import lax
from jax.experimental import pallas as pl
from jax.experimental.pallas import tpu as pltpu
from jax.sharding import PartitionSpec as P

F32 = jnp.float32
BF16 = jnp.bfloat16
I32 = jnp.int32
MESH = pl.DeviceIdType.MESH
DEPTH = 16
NEAR = 4
PLANE = 32


def ring(distance, size):
    return min(distance, size - distance)


Z_STEPS = sorted(range(1, DEPTH), key=lambda step: -ring(step, DEPTH))
M_STEPS = sorted(
    [(x, core, y) for x in range(4) for core in range(2) for y in range(4) if x + core + y > 0],
    key=lambda step: -2 * (ring(step[0], 4) + ring(step[2], 4)) - step[1],
)


def project(params, cam):
    focal = 2400.0
    rotation = cam[:9]
    shift_x, shift_y, shift_z = cam[9:]
    world_x, world_y, world_z = params[0:3]
    view_x = rotation[0] * world_x + rotation[1] * world_y + rotation[2] * world_z + shift_x
    view_y = rotation[3] * world_x + rotation[4] * world_y + rotation[5] * world_z + shift_y
    depth = rotation[6] * world_x + rotation[7] * world_y + rotation[8] * world_z + shift_z
    scales = [jnp.exp(params[3 + number]) for number in range(3)]
    quat_real, quat_i, quat_j, quat_k = params[6:10]
    quat_inv = 1.0 / jnp.sqrt(
        quat_real * quat_real + quat_i * quat_i + quat_j * quat_j + quat_k * quat_k
    )
    quat_real = quat_real * quat_inv
    quat_i = quat_i * quat_inv
    quat_j = quat_j * quat_inv
    quat_k = quat_k * quat_inv
    spin = [
        [
            1.0 - 2.0 * (quat_j * quat_j + quat_k * quat_k),
            2.0 * (quat_i * quat_j - quat_real * quat_k),
            2.0 * (quat_i * quat_k + quat_real * quat_j),
        ],
        [
            2.0 * (quat_i * quat_j + quat_real * quat_k),
            1.0 - 2.0 * (quat_i * quat_i + quat_k * quat_k),
            2.0 * (quat_j * quat_k - quat_real * quat_i),
        ],
        [
            2.0 * (quat_i * quat_k - quat_real * quat_j),
            2.0 * (quat_j * quat_k + quat_real * quat_i),
            1.0 - 2.0 * (quat_i * quat_i + quat_j * quat_j),
        ],
    ]
    shaped = [[spin[row][col] * scales[col] for col in range(3)] for row in range(3)]
    depth_inv = 1.0 / depth
    inv_depth = focal * depth_inv
    screen_x = inv_depth * view_x
    screen_y = inv_depth * view_y
    slope_x = screen_x * depth_inv
    slope_y = screen_y * depth_inv
    jac_top = [inv_depth * rotation[col] - slope_x * rotation[6 + col] for col in range(3)]
    jac_low = [inv_depth * rotation[3 + col] - slope_y * rotation[6 + col] for col in range(3)]
    proj_top = [
        jac_top[0] * shaped[0][col] + jac_top[1] * shaped[1][col] + jac_top[2] * shaped[2][col]
        for col in range(3)
    ]
    proj_low = [
        jac_low[0] * shaped[0][col] + jac_low[1] * shaped[1][col] + jac_low[2] * shaped[2][col]
        for col in range(3)
    ]
    cov_xx = proj_top[0] * proj_top[0] + proj_top[1] * proj_top[1] + proj_top[2] * proj_top[2] + 0.3
    cov_xy = proj_top[0] * proj_low[0] + proj_top[1] * proj_low[1] + proj_top[2] * proj_low[2]
    cov_yy = proj_low[0] * proj_low[0] + proj_low[1] * proj_low[1] + proj_low[2] * proj_low[2] + 0.3
    det_inv = 1.0 / (cov_xx * cov_yy - cov_xy * cov_xy)
    conic_a = cov_yy * det_inv
    conic_b = -cov_xy * det_inv
    conic_c = cov_xx * det_inv
    centre_x = -(rotation[0] * shift_x + rotation[3] * shift_y + rotation[6] * shift_z)
    centre_y = -(rotation[1] * shift_x + rotation[4] * shift_y + rotation[7] * shift_z)
    centre_z = -(rotation[2] * shift_x + rotation[5] * shift_y + rotation[8] * shift_z)
    ray_x = world_x - centre_x
    ray_y = world_y - centre_y
    ray_z = world_z - centre_z
    ray_inv = 1.0 / jnp.sqrt(ray_x * ray_x + ray_y * ray_y + ray_z * ray_z)
    ray_x = ray_x * ray_inv
    ray_y = ray_y * ray_inv
    ray_z = ray_z * ray_inv
    sq_x = ray_x * ray_x
    sq_y = ray_y * ray_y
    sq_z = ray_z * ray_z
    basis = [
        -0.4886025119029199 * ray_y,
        0.4886025119029199 * ray_z,
        -0.4886025119029199 * ray_x,
        1.0925484305920792 * ray_x * ray_y,
        -1.0925484305920792 * ray_y * ray_z,
        0.31539156525252005 * (2.0 * sq_z - sq_x - sq_y),
        -1.0925484305920792 * ray_x * ray_z,
        0.5462742152960396 * (sq_x - sq_y),
        -0.5900435899266435 * ray_y * (3.0 * sq_x - sq_y),
        2.890611442640554 * ray_x * ray_y * ray_z,
        -0.4570457994644658 * ray_y * (4.0 * sq_z - sq_x - sq_y),
        0.3731763325901154 * ray_z * (2.0 * sq_z - 3.0 * sq_x - 3.0 * sq_y),
        -0.4570457994644658 * ray_x * (4.0 * sq_z - sq_x - sq_y),
        1.445305721320277 * ray_z * (sq_x - sq_y),
        -0.5900435899266435 * ray_x * (sq_x - 3.0 * sq_y),
    ]
    colours = []
    for channel in range(3):
        total = 0.5 + 0.28209479177387814 * params[11 + channel]
        for degree in range(1, 16):
            total = total + basis[degree - 1] * params[11 + 3 * degree + channel]
        colours.append(jnp.maximum(total, 0.0))
    return (screen_x + 1920.0, screen_y + 1080.0, conic_a, conic_b, conic_c, *colours)


def iotas(shape):
    return (lax.broadcasted_iota(I32, shape, 0), lax.broadcasted_iota(I32, shape, 1))


def take_lanes(values, lanes):
    return jnp.take_along_axis(
        jnp.broadcast_to(values, lanes.shape), lanes, axis=1, mode="promise_in_bounds"
    )


def lookup(tables, rows, lanes, start=None):
    results = [start] * len(tables)
    for row in range(tables[0].shape[0]):
        here = rows == row
        for number, table in enumerate(tables):
            taken = take_lanes(table[row : row + 1, :], lanes)
            if results[number] is None:
                results[number] = taken
            else:
                results[number] = jnp.where(here, taken, results[number])
    return results


def split2(values):
    high = values.astype(BF16).astype(F32)
    return (high, (values - high).astype(BF16).astype(F32))


def split3(values):
    high = values.astype(BF16).astype(F32)
    rest = values - high
    mid = rest.astype(BF16).astype(F32)
    return (high, mid, (rest - mid).astype(BF16).astype(F32))


def inverse(targets):
    count = targets.shape[0]
    target_row = targets >> 7
    target_lane = targets & 127
    sub8, _ = iotas((8, 128))
    sub128, _ = iotas((128, 128))
    lane = lax.broadcasted_iota(I32, (1, 128), 1).astype(F32)
    left, right = [], []
    for row in range(count):
        match = target_row[row : row + 1, :] == sub8
        low = jnp.where(match, lane, 0.0)
        high = jnp.where(match, float(row + 1), 0.0)
        left.append(jnp.concatenate([low, high], axis=0))
        right.append(jnp.where(target_lane[row : row + 1, :] == sub128, 1.0, 0.0))
    left = jnp.concatenate(left, axis=1).astype(BF16)
    right = jnp.concatenate(right, axis=1).astype(BF16)
    found = nt(left, right).astype(I32)
    return (found[8:16] - 1, found[0:8])


def nt(left, right):
    return lax.dot_general(
        left, right, (((1,), (1,)), ((), ())), preferred_element_type=F32
    )


def nn(left, right):
    return jnp.dot(left, right, preferred_element_type=F32)


def stage(values, bufs):
    packs, plane_out = bufs[0:2]
    _, lane8 = iotas((8, 128))
    _, lane4 = iotas((4, 128))
    quarter8 = lane8 & 3
    for part in range(4):
        spot = part * 32 + (lane8 >> 2)
        for group in range(2):
            packed = take_lanes(values[4 * group], spot)
            for q in range(1, 4):
                packed = jnp.where(quarter8 == q, take_lanes(values[4 * group + q], spot), packed)
            for c in range(2):
                for plane in range(4):
                    row = 4 * c + plane
                    packs[4 * plane + part, pl.ds(2 * group + c, 1)] = packed[row : row + 1]
        last = take_lanes(values[8], spot)
        last = jnp.where((lane4 & 3) == 0, last[0:4], last[4:8])
        for plane in range(4):
            packs[4 * plane + part, pl.ds(4, 1)] = last[plane : plane + 1]

    plane_out[...] = packs[...].reshape(128, 128).T.reshape(PLANE, 4, 128)


def exchange(where_am_i, bufs, meanwhile=lambda: None, between=lambda: None):
    my_z, my_m, z_partners, m_partners = where_am_i
    plane_out, plane_in, depth_out, depth_in, send1, recv1, send2, recv2 = bufs[1:]
    sub8, lane8 = iotas((8, 128))
    for to, device in m_partners:
        pltpu.make_async_remote_copy(
            src_ref=plane_out.at[to],
            dst_ref=plane_in.at[my_m],
            send_sem=send1,
            recv_sem=recv1,
            device_id=device,
            device_id_type=MESH,
        ).start()
    plane_in[my_m] = plane_out[my_m]
    meanwhile()
    plane_all = plane_in.at[pl.ds(0, PLANE - 1)]
    pltpu.make_async_copy(plane_all, plane_all, recv1).wait()
    depth_out[...] = plane_in[...].reshape(128, 128).T.reshape(DEPTH, 8, 128)
    between()
    for to, device in z_partners:
        pltpu.make_async_remote_copy(
            src_ref=depth_out.at[to, pl.ds(0, 5)],
            dst_ref=depth_in.at[pl.ds(pl.multiple_of(my_z * 8, 8), 5)],
            send_sem=send2,
            recv_sem=recv2,
            device_id=device,
            device_id_type=MESH,
        ).start()
    depth_in[pl.ds(pl.multiple_of(my_z * 8, 8), 8), :] = depth_out[my_z]
    pltpu.make_async_copy(plane_all, plane_all, send1).wait()
    depth_all = depth_out.at[pl.ds(0, DEPTH - 1), pl.ds(0, 5)]
    pltpu.make_async_copy(depth_all, depth_all, recv2).wait()
    pltpu.make_async_copy(depth_all, depth_all, send2).wait()

    part8 = lane8 >> 5
    base = (lane8 & 31) << 2
    results = []
    for group in range(2):
        blocks = [
            jnp.concatenate(
                [depth_in[pl.ds(part * 8 + 2 * group + c, 4, stride=32), :] for c in range(2)], axis=0
            )
            for part in range(4)
        ]
        for q in range(4):
            value = take_lanes(blocks[0], base + q)
            for part in range(1, 4):
                value = jnp.where(part8 == part, take_lanes(blocks[part], base + q), value)
            results.append(value)
    spot = base + (sub8 >> 2)
    value = None
    for part in range(4):
        block = depth_in[pl.ds(part * 8 + 4, 4, stride=32), :]
        taken = take_lanes(jnp.concatenate([block, block], axis=0), spot)
        value = taken if value is None else jnp.where(part8 == part, taken, value)
    results.append(value)
    return results


def prepare(ids_ref, list_ref, len_ref, cot_ref, colour_s, coef_s):
    sub4, lane4 = iotas((4, 128))
    low = jnp.concatenate([list_ref[t : t + 1, 0:128] for t in (0, 0, 1, 1)], axis=0)
    high = jnp.concatenate([list_ref[t : t + 1, 128:256] for t in (0, 0, 1, 1)], axis=0)
    spot = 32 * (lane4 & 3) + (sub4 & 1) * 16 + (lane4 >> 3)
    slots = jnp.where((lane4 & 7) < 4, take_lanes(low, spot), take_lanes(high, spot))
    entry = 32 * (lane4 & 7) + (sub4 & 1) * 16 + (lane4 >> 3)
    live = entry < jnp.where(sub4 < 2, len_ref[0, 0, 0], len_ref[0, 0, 1])
    back_row, back_lane = inverse(jnp.where(live, slots, -1))

    first_x = (ids_ref[0, 0, 0] % 240 * 16).astype(F32) + 7.5
    first_y = (ids_ref[0, 0, 0] // 240 * 16).astype(F32) + 7.5
    other_x = (ids_ref[0, 0, 1] % 240 * 16).astype(F32) + 7.5
    other_y = (ids_ref[0, 0, 1] // 240 * 16).astype(F32) + 7.5
    corner = (jnp.where(sub4 < 2, first_x, other_x), jnp.where(sub4 < 2, first_y, other_y))
    colour_s[...] = jnp.zeros_like(colour_s)
    for row in (30, 31):
        coef_s[pl.ds(row, 4, stride=32), :] = jnp.zeros((4, 128), F32)
    row32, pixel = iotas((32, 256))
    local_x = (pixel & 15).astype(F32) - 7.5
    local_y = (pixel >> 4).astype(F32) - 7.5
    terms = [
        local_x * local_x,
        local_y * local_y,
        local_x * local_y,
        local_x,
        local_y,
        jnp.ones_like(local_x),
    ]
    basis = jnp.zeros_like(local_x)
    moments = jnp.zeros_like(local_x)
    for number, term in enumerate(terms):
        basis = jnp.where((row32 >= 3 * number) & (row32 < 3 * number + 3), term, basis)
        moments = jnp.where(row32 == number, term, moments)
    basis = basis.astype(BF16)
    moments = moments[0:16].astype(BF16)
    cot_rows, shades = [], []
    for t in range(2):
        shade = jnp.zeros_like(local_x)
        sums = jnp.zeros_like(local_x)
        for channel in range(3):
            value = cot_ref[channel, 0:1, t * 256 : t * 256 + 256]
            piece_h, piece_l = split2(value)
            start = 18 + 4 * channel
            shade = jnp.where((row32 == start) | (row32 == start + 2), piece_h, shade)
            shade = jnp.where((row32 == start + 1) | (row32 == start + 3), piece_l, shade)
            sums = jnp.where(row32 == channel, piece_h, sums)
            sums = jnp.where(row32 == channel + 8, piece_l, sums)
        cot_rows.append(sums[0:16].astype(BF16))
        shades.append(shade.astype(BF16))
    return (live, slots >> 7, slots & 127, back_row, back_lane, corner, basis, moments, cot_rows, shades)


def render(
    table, prepared, image_ref,
    coef_s, colour_s, power_s, shade_s, alpha_s, keep_s, weight_h, weight_l, after_s, grad_h, grad_l, sum_s, tint_s,
):
    live, slot_row, slot_lane, back_row, back_lane, corner, basis, moments, cot_rows, shades = prepared
    pos_x, pos_y, con_a, con_b, con_c, red, green, blue, log_o = lookup(table, slot_row, slot_lane)
    pos_x = pos_x - corner[0]
    pos_y = pos_y - corner[1]
    slope_x = con_a * pos_x + con_b * pos_y
    slope_y = con_c * pos_y + con_b * pos_x
    level = log_o - 0.5 * (slope_x * pos_x + slope_y * pos_y)
    coefs = [-0.5 * con_a, -0.5 * con_c, -con_b, slope_x, slope_y]
    coefs = [jnp.where(live, value, 0.0) for value in coefs]
    coefs.append(jnp.where(live, level, -1.0e5))
    for number, value in enumerate(coefs):
        for part, piece in enumerate(split3(value)):
            coef_s[pl.ds(3 * number + part, 4, stride=32), :] = piece
    for channel, value in enumerate((red, green, blue)):
        piece_h, piece_l = split2(value)
        for part in range(4):
            coef_s[pl.ds(18 + 4 * channel + part, 4, stride=32), :] = (piece_h, piece_l)[part // 2]
        for block in range(4):
            cols = slice((block % 2) * 128, (block % 2) * 128 + 128)
            at = block // 2 * 16 + channel
            colour_s[at : at + 1, cols] = piece_h[block : block + 1, :]
            colour_s[at + 8 : at + 9, cols] = piece_l[block : block + 1, :]

    for t in range(2):
        left = jnp.concatenate(
            [coef_s[(2 * t + h) * 32 : (2 * t + h) * 32 + 32, :].T for h in range(2)], axis=0
        ).astype(BF16)
        power_s[t * 256 : t * 256 + 256, :] = nn(left, basis)
        shade_s[t * 256 : t * 256 + 256, :] = nn(left, shades[t])

    def forward(step, kept):
        kept = list(kept)
        for t in range(2):
            for inner in range(4):
                rows = pl.ds(pl.multiple_of(t * 256 + step * 32 + inner * 8, 8), 8)
                alpha = jnp.exp(power_s[rows, :])
                alpha_s[rows, :] = alpha
                keep_s[rows, :] = kept[t]
                kept[t] = kept[t] * (1.0 - alpha)
        return tuple(kept)

    ones = jnp.ones((8, 256), F32)
    kept = (ones, ones)
    for step in range(8):
        kept = forward(step, kept)
    sub_k, _ = iotas((8, 256))

    def ahead(values):
        result = jnp.where(sub_k >= 1, pltpu.roll(values, 1, 0), 1.0)
        for shift in (1, 2, 4):
            result = result * jnp.where(sub_k >= shift, pltpu.roll(result, shift, 0), 1.0)
        return result

    def behind(values):
        result = jnp.where(sub_k < 7, pltpu.roll(values, 7, 0), 0.0)
        for shift in (1, 2, 4):
            result = result + jnp.where(sub_k < 8 - shift, pltpu.roll(result, 8 - shift, 0), 0.0)
        return result

    entering = [ahead(kept[t]) for t in range(2)]

    def backward(step, sums):
        sums = list(sums)
        for t in range(2):
            for pair in (1, 0):
                start = t * 256 + (7 - step) * 32 + pair * 16
                weights = [None, None]
                for half in (1, 0):
                    rows = pl.ds(pl.multiple_of(start + half * 8, 8), 8)
                    weight = keep_s[rows, :] * entering[t] * alpha_s[rows, :]
                    gain = weight * shade_s[rows, :]
                    weights[half] = weight
                    after_s[rows, :] = sums[t]
                    power_s[rows, :] = gain
                    sums[t] = sums[t] + gain
                weight = jnp.concatenate(weights, axis=0)
                rows = pl.ds(pl.multiple_of(start, 16), 16)
                piece = weight.astype(BF16)
                weight_h[rows, :] = piece
                weight_l[rows, :] = (weight - piece.astype(F32)).astype(BF16)
        return tuple(sums)

    zeros = jnp.zeros((8, 256), F32)
    sums = (zeros, zeros)
    for step in range(8):
        sums = backward(step, sums)
    leaving = [behind(sums[t]) for t in range(2)]
    leaving = [jnp.concatenate([value, value], axis=0) for value in leaving]

    def slopes(step, carry):
        for t in range(2):
            for pair in range(2):
                rows = pl.ds(pl.multiple_of(t * 256 + step * 32 + pair * 16, 16), 16)
                alpha = alpha_s[rows, :]
                ratio = alpha / (1.0 - alpha)
                grad = power_s[rows, :] - ratio * (after_s[rows, :] + leaving[t])
                piece = grad.astype(BF16)
                grad_h[rows, :] = piece
                grad_l[rows, :] = (grad - piece.astype(F32)).astype(BF16)
        return carry

    for step in range(8):
        slopes(step, 0)

    for t in range(2):
        rows = slice(t * 256, t * 256 + 256)
        tints = colour_s[t * 16 : t * 16 + 16, :].astype(BF16)
        picture = nn(tints, weight_h[rows, :]) + nn(tints, weight_l[rows, :])
        picture = picture[0:8] + picture[8:16]
        for channel in range(3):
            image_ref[channel, 0:1, rows] = picture[channel : channel + 1, :]
        total = nt(moments, grad_h[rows, :]) + nt(moments, grad_l[rows, :])
        tint = nt(cot_rows[t], weight_h[rows, :]) + nt(cot_rows[t], weight_l[rows, :])
        tint = tint[0:8] + tint[8:16]
        for h in range(2):
            cols = slice(h * 128, h * 128 + 128)
            at = (2 * t + h) * 8
            sum_s[at : at + 8, :] = total[0:8, cols]
            tint_s[at : at + 8, :] = tint[:, cols]

    sum_xx, sum_yy, sum_xy, sum_x, sum_y, sum_1 = [
        sum_s[pl.ds(number, 4, stride=8), :] for number in range(6)
    ]
    tints = [tint_s[pl.ds(number, 4, stride=8), :] for number in range(3)]
    first_mx = sum_x - pos_x * sum_1
    first_my = sum_y - pos_y * sum_1
    grads = [
        con_a * first_mx + con_b * first_my,
        con_c * first_my + con_b * first_mx,
        -0.5 * (sum_xx - pos_x * (sum_x + first_mx)),
        -(sum_xy - pos_x * sum_y - pos_y * first_mx),
        -0.5 * (sum_yy - pos_y * (sum_y + first_my)),
        *tints,
        sum_1,
    ]
    return lookup(grads, back_row, back_lane, jnp.zeros((8, 128), F32))


def kernel(
    gauss_hbm, cam_hbm, send_hbm, ids_hbm, list_hbm, len_hbm, cot_hbm, image_ref, out_ref,
    gauss_ref, cam_ref, send_ref, ids_ref, list_ref, len_ref, cot_ref, in_sem, far_sem, spread, *scratch,
):
    there, back, work = scratch[0:9], scratch[9:18], scratch[18:]
    tile = lax.axis_index("tile")
    view = lax.axis_index("view")
    my_z = tile // 8
    mine = lax.rem(tile, 8)
    my_x, my_core = mine // 2, lax.rem(mine, 2)
    my_m = mine * 4 + view
    z_partners, m_partners = [], []
    for step in Z_STEPS:
        to = lax.rem(my_z + step, DEPTH)
        z_partners.append((to, (to * 8 + mine, view)))
    for x, core, y in M_STEPS:
        place = lax.rem(my_x + x, 4) * 2 + lax.rem(my_core + core, 2)
        row = lax.rem(view + y, 4)
        m_partners.append((place * 4 + row, (my_z * 8 + place, row)))
    where_am_i = (my_z, my_m, z_partners, m_partners)

    barrier = pltpu.get_barrier_semaphore()

    inputs = [
        pltpu.make_async_copy(source, target, in_sem.at[number])
        for number, (source, target) in enumerate(
            [
                (send_hbm, send_ref),
                (gauss_hbm, gauss_ref),
                (cam_hbm, cam_ref),
                (ids_hbm, ids_ref),
                (list_hbm, list_ref),
                (len_hbm, len_ref),
                (cot_hbm, cot_ref),
            ]
        )
    ]
    for copy in inputs[0:2]:
        copy.start()
    near = [entry for step, entry in zip(Z_STEPS, z_partners) if ring(step, DEPTH) <= NEAR]
    for _, device in near + m_partners:
        pl.semaphore_signal(barrier, inc=1, device_id=device, device_id_type=MESH)
    for copy in inputs[2:]:
        copy.start()
    inputs[0].wait()

    sub8, lane8 = iotas((8, 128))
    spot = (sub8 & 3) * 32 + (lane8 >> 2)
    targets = None
    for number in range(4):
        row = jnp.where(sub8 < 4, send_ref[number : number + 1, :], send_ref[4 + number : 5 + number, :])
        taken = take_lanes(row, spot)
        targets = taken if targets is None else jnp.where((lane8 & 3) == number, taken, targets)
    slot_row, slot_lane = inverse(targets)
    sent = slot_row >= 0
    for copy in inputs[1:]:
        copy.wait()
    cam = []
    for number in range(12):
        value = jnp.full((8, 128), cam_ref[0, number], F32)
        for other in range(1, 4):
            value = jnp.where((slot_lane & 3) == other, cam_ref[other, number], value)
        cam.append(value)

    for block in range(8):
        spread[pl.ds(block, 59, stride=8), :] = gauss_ref[:, block * 128 : block * 128 + 128]

    def read_params():
        return [spread[8 * number : 8 * number + 8, :] for number in range(59)]

    params = read_params()
    splats, pull_back = jax.vjp(lambda values: project(values, cam), params)
    logit = params[10]
    splats = [*splats, jnp.minimum(logit, 0.0) - jnp.log1p(jnp.exp(-jnp.abs(logit)))]
    logit_slope = 1.0 / (1.0 + jnp.exp(logit))
    chosen = jnp.maximum(targets, 0)
    outgoing = lookup(splats, chosen >> 7, chosen & 127)

    stage(outgoing, there)
    prepared = prepare(ids_ref, list_ref, len_ref, cot_ref, work[1], work[0])

    pl.semaphore_wait(barrier, PLANE - 1 + 2 * NEAR)
    for step, (_, device) in zip(Z_STEPS, z_partners):
        if ring(step, DEPTH) == NEAR:
            pl.semaphore_signal(far_sem, inc=1, device_id=device, device_id_type=MESH)
    arrived = exchange(where_am_i, there, between=lambda: pl.semaphore_wait(far_sem, 2))
    slot_grads = render(arrived, prepared, image_ref, *work)
    stage(slot_grads, back)
    returned = exchange(where_am_i, back)

    grads = lookup(returned, slot_row, slot_lane, jnp.zeros((8, 128), F32))
    (param_grads,) = pull_back(tuple(grads[0:8]))
    for number, value in enumerate(param_grads):
        if number == 10:
            value = grads[8] * logit_slope
        spread[8 * number : 8 * number + 8, :] = jnp.where(sent, value, 0.0)
    for block in range(8):
        out_ref[:, block * 128 : block * 128 + 128] = spread[pl.ds(block, 59, stride=8), :]


def store(image_ref, grads_ref, image_out, grads_out, sems):
    copies = [
        pltpu.make_async_copy(grads_ref, grads_out, sems.at[0]),
        pltpu.make_async_copy(image_ref, image_out, sems.at[1]),
    ]
    for copy in copies:
        copy.start()
    for copy in copies:
        copy.wait()


def exchange_scratch():
    return [
        pltpu.VMEM((DEPTH, 8, 128), F32),
        pltpu.VMEM((PLANE, 4, 128), F32),
        pltpu.VMEM((PLANE, 4, 128), F32),
        pltpu.VMEM((DEPTH, 8, 128), F32),
        pltpu.VMEM((128, 128), F32),
        pltpu.SemaphoreType.DMA,
        pltpu.SemaphoreType.DMA,
        pltpu.SemaphoreType.DMA,
        pltpu.SemaphoreType.DMA,
    ]


def render_scratch():
    return [
        pltpu.VMEM((128, 128), F32),
        pltpu.VMEM((32, 256), F32),
        pltpu.VMEM((512, 256), F32),
        pltpu.VMEM((512, 256), F32),
        pltpu.VMEM((512, 256), F32),
        pltpu.VMEM((512, 256), F32),
        pltpu.VMEM((512, 256), BF16),
        pltpu.VMEM((512, 256), BF16),
        pltpu.VMEM((512, 256), F32),
        pltpu.VMEM((512, 256), BF16),
        pltpu.VMEM((512, 256), BF16),
        pltpu.VMEM((32, 128), F32),
        pltpu.VMEM((32, 128), F32),
    ]


def per_device(gaussians, camera, send_index, tile_ids, tile_lists, tile_lengths, pixel_grad):
    sends = jnp.transpose(send_index, (0, 1, 3, 2)).reshape(8, 128)
    lists = tile_lists.reshape(2, 256)
    vmem = pl.BlockSpec(memory_space=pltpu.VMEM)
    hbm = pl.BlockSpec(memory_space=pltpu.HBM)
    operands = [
        pltpu.with_memory_space_constraint(value, pltpu.HBM)
        for value in (gaussians, camera, sends, tile_ids, lists, tile_lengths, pixel_grad)
    ]
    results_shape = (
        jax.ShapeDtypeStruct((3, 1, 512), F32),
        jax.ShapeDtypeStruct((59, 1024), F32),
    )
    results = pl.pallas_call(
        kernel,
        out_shape=results_shape,
        in_specs=[hbm] * 7,
        out_specs=(vmem, vmem),
        scratch_shapes=[
            pltpu.VMEM((59, 1024), F32),
            pltpu.SMEM((4, 12), F32),
            pltpu.VMEM((8, 128), I32),
            pltpu.SMEM((1, 1, 2), I32),
            pltpu.VMEM((2, 256), I32),
            pltpu.SMEM((1, 1, 2), I32),
            pltpu.VMEM((3, 1, 512), F32),
            pltpu.SemaphoreType.DMA((7,)),
            pltpu.SemaphoreType.REGULAR,
            pltpu.VMEM((480, 128), F32),
            *exchange_scratch(),
            *exchange_scratch(),
            *render_scratch(),
        ],
        compiler_params=pltpu.CompilerParams(
            collective_id=0, has_side_effects=True, vmem_limit_bytes=32 * 1024 * 1024
        ),
    )(*operands)
    return tuple(
        pl.pallas_call(
            store,
            out_shape=results_shape,
            in_specs=[vmem, vmem],
            out_specs=(hbm, hbm),
            scratch_shapes=[pltpu.SemaphoreType.DMA((2,))],
            compiler_params=pltpu.CompilerParams(vmem_limit_bytes=1024 * 1024),
        )(*results)
    )


def solution(mesh):
    return jax.shard_map(
        per_device,
        mesh=mesh,
        in_specs=(
            P(None, ("tile", "view")),
            P(),
            P(("tile", "view"), None, None, None),
            P("view", "tile", None),
            P("view", "tile", None, None),
            P("view", "tile", None),
            P(None, "view", "tile"),
        ),
        out_specs=(P(None, "view", "tile"), P(None, ("tile", "view"))),
        check_vma=False,
    )
```

```python
import jax
import jax.numpy as jnp
from jax import lax
from jax.experimental import pallas as pl
from jax.experimental.pallas import tpu as pltpu
from jax.sharding import PartitionSpec as P

F32 = jnp.float32
BF16 = jnp.bfloat16
I32 = jnp.int32
MESH = pl.DeviceIdType.MESH
DEPTH = 16
NEAR = 4
PLANE = 32


def ring(distance, size):
    return min(distance, size - distance)


Z_STEPS = sorted(range(1, DEPTH), key=lambda step: -ring(step, DEPTH))
M_STEPS = sorted(
    [(x, core, y) for x in range(4) for core in range(2) for y in range(4) if x + core + y > 0],
    key=lambda step: -2 * (ring(step[0], 4) + ring(step[2], 4)) - step[1],
)


def project(params, cam):
    focal = 2400.0
    rotation = cam[:9]
    shift_x, shift_y, shift_z = cam[9:]
    world_x, world_y, world_z = params[0:3]
    view_x = rotation[0] * world_x + rotation[1] * world_y + rotation[2] * world_z + shift_x
    view_y = rotation[3] * world_x + rotation[4] * world_y + rotation[5] * world_z + shift_y
    depth = rotation[6] * world_x + rotation[7] * world_y + rotation[8] * world_z + shift_z
    scales = [jnp.exp(params[3 + number]) for number in range(3)]
    quat_real, quat_i, quat_j, quat_k = params[6:10]
    quat_inv = 1.0 / jnp.sqrt(
        quat_real * quat_real + quat_i * quat_i + quat_j * quat_j + quat_k * quat_k
    )
    quat_real = quat_real * quat_inv
    quat_i = quat_i * quat_inv
    quat_j = quat_j * quat_inv
    quat_k = quat_k * quat_inv
    spin = [
        [
            1.0 - 2.0 * (quat_j * quat_j + quat_k * quat_k),
            2.0 * (quat_i * quat_j - quat_real * quat_k),
            2.0 * (quat_i * quat_k + quat_real * quat_j),
        ],
        [
            2.0 * (quat_i * quat_j + quat_real * quat_k),
            1.0 - 2.0 * (quat_i * quat_i + quat_k * quat_k),
            2.0 * (quat_j * quat_k - quat_real * quat_i),
        ],
        [
            2.0 * (quat_i * quat_k - quat_real * quat_j),
            2.0 * (quat_j * quat_k + quat_real * quat_i),
            1.0 - 2.0 * (quat_i * quat_i + quat_j * quat_j),
        ],
    ]
    shaped = [[spin[row][col] * scales[col] for col in range(3)] for row in range(3)]
    depth_inv = 1.0 / depth
    inv_depth = focal * depth_inv
    screen_x = inv_depth * view_x
    screen_y = inv_depth * view_y
    slope_x = screen_x * depth_inv
    slope_y = screen_y * depth_inv
    jac_top = [inv_depth * rotation[col] - slope_x * rotation[6 + col] for col in range(3)]
    jac_low = [inv_depth * rotation[3 + col] - slope_y * rotation[6 + col] for col in range(3)]
    proj_top = [
        jac_top[0] * shaped[0][col] + jac_top[1] * shaped[1][col] + jac_top[2] * shaped[2][col]
        for col in range(3)
    ]
    proj_low = [
        jac_low[0] * shaped[0][col] + jac_low[1] * shaped[1][col] + jac_low[2] * shaped[2][col]
        for col in range(3)
    ]
    cov_xx = proj_top[0] * proj_top[0] + proj_top[1] * proj_top[1] + proj_top[2] * proj_top[2] + 0.3
    cov_xy = proj_top[0] * proj_low[0] + proj_top[1] * proj_low[1] + proj_top[2] * proj_low[2]
    cov_yy = proj_low[0] * proj_low[0] + proj_low[1] * proj_low[1] + proj_low[2] * proj_low[2] + 0.3
    det_inv = 1.0 / (cov_xx * cov_yy - cov_xy * cov_xy)
    conic_a = cov_yy * det_inv
    conic_b = -cov_xy * det_inv
    conic_c = cov_xx * det_inv
    centre_x = -(rotation[0] * shift_x + rotation[3] * shift_y + rotation[6] * shift_z)
    centre_y = -(rotation[1] * shift_x + rotation[4] * shift_y + rotation[7] * shift_z)
    centre_z = -(rotation[2] * shift_x + rotation[5] * shift_y + rotation[8] * shift_z)
    ray_x = world_x - centre_x
    ray_y = world_y - centre_y
    ray_z = world_z - centre_z
    ray_inv = 1.0 / jnp.sqrt(ray_x * ray_x + ray_y * ray_y + ray_z * ray_z)
    ray_x = ray_x * ray_inv
    ray_y = ray_y * ray_inv
    ray_z = ray_z * ray_inv
    sq_x = ray_x * ray_x
    sq_y = ray_y * ray_y
    sq_z = ray_z * ray_z
    basis = [
        -0.4886025119029199 * ray_y,
        0.4886025119029199 * ray_z,
        -0.4886025119029199 * ray_x,
        1.0925484305920792 * ray_x * ray_y,
        -1.0925484305920792 * ray_y * ray_z,
        0.31539156525252005 * (2.0 * sq_z - sq_x - sq_y),
        -1.0925484305920792 * ray_x * ray_z,
        0.5462742152960396 * (sq_x - sq_y),
        -0.5900435899266435 * ray_y * (3.0 * sq_x - sq_y),
        2.890611442640554 * ray_x * ray_y * ray_z,
        -0.4570457994644658 * ray_y * (4.0 * sq_z - sq_x - sq_y),
        0.3731763325901154 * ray_z * (2.0 * sq_z - 3.0 * sq_x - 3.0 * sq_y),
        -0.4570457994644658 * ray_x * (4.0 * sq_z - sq_x - sq_y),
        1.445305721320277 * ray_z * (sq_x - sq_y),
        -0.5900435899266435 * ray_x * (sq_x - 3.0 * sq_y),
    ]
    colours = []
    for channel in range(3):
        total = 0.5 + 0.28209479177387814 * params[11 + channel]
        for degree in range(1, 16):
            total = total + basis[degree - 1] * params[11 + 3 * degree + channel]
        colours.append(jnp.maximum(total, 0.0))
    return (screen_x + 1920.0, screen_y + 1080.0, conic_a, conic_b, conic_c, *colours)


def iotas(shape):
    return (lax.broadcasted_iota(I32, shape, 0), lax.broadcasted_iota(I32, shape, 1))


def take_lanes(values, lanes):
    return jnp.take_along_axis(
        jnp.broadcast_to(values, lanes.shape), lanes, axis=1, mode="promise_in_bounds"
    )


def lookup(tables, rows, lanes, start=None):
    results = [start] * len(tables)
    for row in range(tables[0].shape[0]):
        here = rows == row
        for number, table in enumerate(tables):
            taken = take_lanes(table[row : row + 1, :], lanes)
            if results[number] is None:
                results[number] = taken
            else:
                results[number] = jnp.where(here, taken, results[number])
    return results


def split2(values):
    high = values.astype(BF16).astype(F32)
    return (high, (values - high).astype(BF16).astype(F32))


def split3(values):
    high = values.astype(BF16).astype(F32)
    rest = values - high
    mid = rest.astype(BF16).astype(F32)
    return (high, mid, (rest - mid).astype(BF16).astype(F32))


def inverse(targets):
    count = targets.shape[0]
    target_row = targets >> 7
    target_lane = targets & 127
    sub8, _ = iotas((8, 128))
    sub128, _ = iotas((128, 128))
    lane = lax.broadcasted_iota(I32, (1, 128), 1).astype(F32)
    left, right = [], []
    for row in range(count):
        match = target_row[row : row + 1, :] == sub8
        low = jnp.where(match, lane, 0.0)
        high = jnp.where(match, float(row + 1), 0.0)
        left.append(jnp.concatenate([low, high], axis=0))
        right.append(jnp.where(target_lane[row : row + 1, :] == sub128, 1.0, 0.0))
    left = jnp.concatenate(left, axis=1).astype(BF16)
    right = jnp.concatenate(right, axis=1).astype(BF16)
    found = nt(left, right).astype(I32)
    return (found[8:16] - 1, found[0:8])


def nt(left, right):
    return lax.dot_general(
        left, right, (((1,), (1,)), ((), ())), preferred_element_type=F32
    )


def nn(left, right):
    return jnp.dot(left, right, preferred_element_type=F32)


def stage(values, bufs):
    packs, plane_out = bufs[0:2]
    _, lane8 = iotas((8, 128))
    _, lane4 = iotas((4, 128))
    quarter8 = lane8 & 3
    for part in range(4):
        spot = part * 32 + (lane8 >> 2)
        for group in range(2):
            packed = take_lanes(values[4 * group], spot)
            for q in range(1, 4):
                packed = jnp.where(quarter8 == q, take_lanes(values[4 * group + q], spot), packed)
            for c in range(2):
                for plane in range(4):
                    row = 4 * c + plane
                    packs[4 * plane + part, pl.ds(2 * group + c, 1)] = packed[row : row + 1]
        last = take_lanes(values[8], spot)
        last = jnp.where((lane4 & 3) == 0, last[0:4], last[4:8])
        for plane in range(4):
            packs[4 * plane + part, pl.ds(4, 1)] = last[plane : plane + 1]

    plane_out[0:PLANE] = packs[0:DEPTH].reshape(128, 128).T.reshape(PLANE, 4, 128)


def exchange(where_am_i, bufs, meanwhile=lambda: None, between=lambda: None):
    my_z, my_m, z_partners, m_partners = where_am_i
    plane_out, plane_in, depth_out, depth_in, send1, recv1, send2, recv2 = bufs[1:]
    sub8, lane8 = iotas((8, 128))
    for to, device in m_partners:
        pltpu.make_async_remote_copy(
            src_ref=plane_out.at[to],
            dst_ref=plane_in.at[my_m],
            send_sem=send1,
            recv_sem=recv1,
            device_id=device,
            device_id_type=MESH,
        ).start()
    plane_in[my_m] = plane_out[my_m]
    meanwhile()
    plane_all = plane_in.at[pl.ds(0, PLANE - 1)]
    pltpu.make_async_copy(plane_all, plane_all, recv1).wait()
    depth_out[...] = plane_in[0:PLANE].reshape(128, 128).T.reshape(DEPTH, 8, 128)
    between()
    for to, device in z_partners:
        pltpu.make_async_remote_copy(
            src_ref=depth_out.at[to, pl.ds(0, 5)],
            dst_ref=depth_in.at[pl.ds(pl.multiple_of(my_z * 8, 8), 5)],
            send_sem=send2,
            recv_sem=recv2,
            device_id=device,
            device_id_type=MESH,
        ).start()
    depth_in[pl.ds(pl.multiple_of(my_z * 8, 8), 8), :] = depth_out[my_z]
    pltpu.make_async_copy(plane_all, plane_all, send1).wait()
    depth_all = depth_out.at[pl.ds(0, DEPTH - 1), pl.ds(0, 5)]
    pltpu.make_async_copy(depth_all, depth_all, recv2).wait()
    pltpu.make_async_copy(depth_all, depth_all, send2).wait()

    part8 = lane8 >> 5
    base = (lane8 & 31) << 2
    results = []
    for group in range(2):
        blocks = [
            jnp.concatenate(
                [depth_in[pl.ds(part * 8 + 2 * group + c, 4, stride=32), :] for c in range(2)], axis=0
            )
            for part in range(4)
        ]
        for q in range(4):
            value = take_lanes(blocks[0], base + q)
            for part in range(1, 4):
                value = jnp.where(part8 == part, take_lanes(blocks[part], base + q), value)
            results.append(value)
    spot = base + (sub8 >> 2)
    value = None
    for part in range(4):
        block = depth_in[pl.ds(part * 8 + 4, 4, stride=32), :]
        taken = take_lanes(jnp.concatenate([block, block], axis=0), spot)
        value = taken if value is None else jnp.where(part8 == part, taken, value)
    results.append(value)
    return results


def prepare(ids_ref, list_ref, len_ref, cot_ref, colour_s, coef_s):
    sub4, lane4 = iotas((4, 128))
    low = jnp.concatenate([list_ref[t : t + 1, 0:128] for t in (0, 0, 1, 1)], axis=0)
    high = jnp.concatenate([list_ref[t : t + 1, 128:256] for t in (0, 0, 1, 1)], axis=0)
    spot = 32 * (lane4 & 3) + (sub4 & 1) * 16 + (lane4 >> 3)
    slots = jnp.where((lane4 & 7) < 4, take_lanes(low, spot), take_lanes(high, spot))
    entry = 32 * (lane4 & 7) + (sub4 & 1) * 16 + (lane4 >> 3)
    live = entry < jnp.where(sub4 < 2, len_ref[0, 0, 0], len_ref[0, 0, 1])
    back_row, back_lane = inverse(jnp.where(live, slots, -1))

    first_x = (ids_ref[0, 0, 0] % 240 * 16).astype(F32) + 7.5
    first_y = (ids_ref[0, 0, 0] // 240 * 16).astype(F32) + 7.5
    other_x = (ids_ref[0, 0, 1] % 240 * 16).astype(F32) + 7.5
    other_y = (ids_ref[0, 0, 1] // 240 * 16).astype(F32) + 7.5
    corner = (jnp.where(sub4 < 2, first_x, other_x), jnp.where(sub4 < 2, first_y, other_y))
    colour_s[...] = jnp.zeros_like(colour_s)
    for row in (30, 31):
        coef_s[pl.ds(row, 4, stride=32), :] = jnp.zeros((4, 128), F32)
    row32, pixel = iotas((32, 256))
    local_x = (pixel & 15).astype(F32) - 7.5
    local_y = (pixel >> 4).astype(F32) - 7.5
    terms = [
        local_x * local_x,
        local_y * local_y,
        local_x * local_y,
        local_x,
        local_y,
        jnp.ones_like(local_x),
    ]
    basis = jnp.zeros_like(local_x)
    moments = jnp.zeros_like(local_x)
    for number, term in enumerate(terms):
        basis = jnp.where((row32 >= 3 * number) & (row32 < 3 * number + 3), term, basis)
        moments = jnp.where(row32 == number, term, moments)
    basis = basis.astype(BF16)
    moments = moments[0:16].astype(BF16)
    cot_rows, shades = [], []
    for t in range(2):
        shade = jnp.zeros_like(local_x)
        sums = jnp.zeros_like(local_x)
        for channel in range(3):
            value = cot_ref[channel, 0:1, t * 256 : t * 256 + 256]
            piece_h, piece_l = split2(value)
            start = 18 + 4 * channel
            shade = jnp.where((row32 == start) | (row32 == start + 2), piece_h, shade)
            shade = jnp.where((row32 == start + 1) | (row32 == start + 3), piece_l, shade)
            sums = jnp.where(row32 == channel, piece_h, sums)
            sums = jnp.where(row32 == channel + 8, piece_l, sums)
        cot_rows.append(sums[0:16].astype(BF16))
        shades.append(shade.astype(BF16))
    return (live, slots >> 7, slots & 127, back_row, back_lane, corner, basis, moments, cot_rows, shades)


def render(
    table, prepared, image_ref,
    coef_s, colour_s, power_s, shade_s, alpha_s, keep_s, weight_h, weight_l, after_s, grad_h, grad_l, sum_s, tint_s,
):
    live, slot_row, slot_lane, back_row, back_lane, corner, basis, moments, cot_rows, shades = prepared
    pos_x, pos_y, con_a, con_b, con_c, red, green, blue, log_o = lookup(table, slot_row, slot_lane)
    pos_x = pos_x - corner[0]
    pos_y = pos_y - corner[1]
    slope_x = con_a * pos_x + con_b * pos_y
    slope_y = con_c * pos_y + con_b * pos_x
    level = log_o - 0.5 * (slope_x * pos_x + slope_y * pos_y)
    coefs = [-0.5 * con_a, -0.5 * con_c, -con_b, slope_x, slope_y]
    coefs = [jnp.where(live, value, 0.0) for value in coefs]
    coefs.append(jnp.where(live, level, -1.0e5))
    for number, value in enumerate(coefs):
        for part, piece in enumerate(split3(value)):
            coef_s[pl.ds(3 * number + part, 4, stride=32), :] = piece
    for channel, value in enumerate((red, green, blue)):
        piece_h, piece_l = split2(value)
        for part in range(4):
            coef_s[pl.ds(18 + 4 * channel + part, 4, stride=32), :] = (piece_h, piece_l)[part // 2]
        for block in range(4):
            cols = slice((block % 2) * 128, (block % 2) * 128 + 128)
            at = block // 2 * 16 + channel
            colour_s[at : at + 1, cols] = piece_h[block : block + 1, :]
            colour_s[at + 8 : at + 9, cols] = piece_l[block : block + 1, :]

    for t in range(2):
        left = jnp.concatenate(
            [coef_s[(2 * t + h) * 32 : (2 * t + h) * 32 + 32, :].T for h in range(2)], axis=0
        ).astype(BF16)
        power_s[t * 256 : t * 256 + 256, :] = nn(left, basis)
        shade_s[t * 256 : t * 256 + 256, :] = nn(left, shades[t])

    sub_k, _ = iotas((8, 256))

    def ahead(values):
        result = jnp.where(sub_k >= 1, pltpu.roll(values, 1, 0), 1.0)
        for shift in (1, 2, 4):
            result = result * jnp.where(sub_k >= shift, pltpu.roll(result, shift, 0), 1.0)
        return result

    def behind(values):
        result = jnp.where(sub_k < 7, pltpu.roll(values, 7, 0), 0.0)
        for shift in (1, 2, 4):
            result = result + jnp.where(sub_k < 8 - shift, pltpu.roll(result, 8 - shift, 0), 0.0)
        return result

    def forward(t):
        kept = jnp.ones((8, 256), F32)
        for block in range(32):
            rows = slice(t * 256 + block * 8, t * 256 + block * 8 + 8)
            alpha = jnp.exp(power_s[rows, :])
            alpha_s[rows, :] = alpha
            keep_s[rows, :] = kept
            kept = kept * (1.0 - alpha)
        return ahead(kept)

    def backward(t, entering):
        total = jnp.zeros((8, 256), F32)
        for pair in reversed(range(16)):
            start = t * 256 + pair * 16
            weights = [None, None]
            for half in (1, 0):
                rows = slice(start + half * 8, start + half * 8 + 8)
                weight = keep_s[rows, :] * entering * alpha_s[rows, :]
                gain = weight * shade_s[rows, :]
                weights[half] = weight
                after_s[rows, :] = total
                power_s[rows, :] = gain
                total = total + gain
            weight = jnp.concatenate(weights, axis=0)
            rows = slice(start, start + 16)
            piece = weight.astype(BF16)
            weight_h[rows, :] = piece
            weight_l[rows, :] = (weight - piece.astype(F32)).astype(BF16)
        return behind(total)

    def slopes(t, leaving):
        leaving = jnp.concatenate([leaving, leaving], axis=0)
        for pair in range(16):
            rows = slice(t * 256 + pair * 16, t * 256 + pair * 16 + 16)
            alpha = alpha_s[rows, :]
            ratio = alpha / (1.0 - alpha)
            grad = power_s[rows, :] - ratio * (after_s[rows, :] + leaving)
            piece = grad.astype(BF16)
            grad_h[rows, :] = piece
            grad_l[rows, :] = (grad - piece.astype(F32)).astype(BF16)

    def paint(t):
        rows = slice(t * 256, t * 256 + 256)
        tints = colour_s[t * 16 : t * 16 + 16, :].astype(BF16)
        picture = nn(tints, weight_h[rows, :]) + nn(tints, weight_l[rows, :])
        picture = picture[0:8] + picture[8:16]
        for channel in range(3):
            image_ref[channel, 0:1, rows] = picture[channel : channel + 1, :]
        tint = nt(cot_rows[t], weight_h[rows, :]) + nt(cot_rows[t], weight_l[rows, :])
        tint = tint[0:8] + tint[8:16]
        for h in range(2):
            at = (2 * t + h) * 8
            tint_s[at : at + 8, :] = tint[:, h * 128 : h * 128 + 128]

    def gather_moments(t):
        rows = slice(t * 256, t * 256 + 256)
        total = nt(moments, grad_h[rows, :]) + nt(moments, grad_l[rows, :])
        for h in range(2):
            at = (2 * t + h) * 8
            sum_s[at : at + 8, :] = total[0:8, h * 128 : h * 128 + 128]

    entering = [forward(t) for t in range(2)]
    leaving = []
    for t in range(2):
        leaving.append(backward(t, entering[t]))
        paint(t)
    for t in range(2):
        slopes(t, leaving[t])
        gather_moments(t)
    sum_xx, sum_yy, sum_xy, sum_x, sum_y, sum_1 = [
        sum_s[pl.ds(number, 4, stride=8), :] for number in range(6)
    ]
    tints = [tint_s[pl.ds(number, 4, stride=8), :] for number in range(3)]
    first_mx = sum_x - pos_x * sum_1
    first_my = sum_y - pos_y * sum_1
    grads = [
        con_a * first_mx + con_b * first_my,
        con_c * first_my + con_b * first_mx,
        -0.5 * (sum_xx - pos_x * (sum_x + first_mx)),
        -(sum_xy - pos_x * sum_y - pos_y * first_mx),
        -0.5 * (sum_yy - pos_y * (sum_y + first_my)),
        *tints,
        sum_1,
    ]
    return lookup(grads, back_row, back_lane, jnp.zeros((8, 128), F32))


def kernel(
    gauss_hbm, cam_hbm, send_hbm, ids_hbm, list_hbm, len_hbm, cot_hbm, image_ref, out_ref,
    gauss_ref, cam_ref, send_ref, ids_ref, list_ref, len_ref, cot_ref, in_sem, far_sem, spread, *scratch,
):
    there, back, work = scratch[0:9], scratch[9:18], scratch[18:]
    tile = lax.axis_index("tile")
    view = lax.axis_index("view")
    my_z = tile // 8
    mine = lax.rem(tile, 8)
    my_x, my_core = mine // 2, lax.rem(mine, 2)
    my_m = mine * 4 + view
    z_partners, m_partners = [], []
    for step in Z_STEPS:
        to = lax.rem(my_z + step, DEPTH)
        z_partners.append((to, (to * 8 + mine, view)))
    for x, core, y in M_STEPS:
        place = lax.rem(my_x + x, 4) * 2 + lax.rem(my_core + core, 2)
        row = lax.rem(view + y, 4)
        m_partners.append((place * 4 + row, (my_z * 8 + place, row)))
    where_am_i = (my_z, my_m, z_partners, m_partners)

    barrier = pltpu.get_barrier_semaphore()

    near = [entry for step, entry in zip(Z_STEPS, z_partners) if ring(step, DEPTH) <= NEAR]
    for _, device in near + m_partners:
        pl.semaphore_signal(barrier, inc=1, device_id=device, device_id_type=MESH)

    inputs = [
        pltpu.make_async_copy(source, target, in_sem.at[number])
        for number, (source, target) in enumerate(
            [
                (send_hbm, send_ref),
                (gauss_hbm, gauss_ref),
                (cam_hbm, cam_ref),
                (ids_hbm, ids_ref),
                (list_hbm, list_ref),
                (len_hbm, len_ref),
                (cot_hbm, cot_ref.at[pl.ds(0, 3)]),
            ]
        )
    ]
    for copy in inputs:
        copy.start()
    inputs[0].wait()

    sub8, lane8 = iotas((8, 128))
    spot = (sub8 & 3) * 32 + (lane8 >> 2)
    targets = None
    for number in range(4):
        row = jnp.where(sub8 < 4, send_ref[number : number + 1, :], send_ref[4 + number : 5 + number, :])
        taken = take_lanes(row, spot)
        targets = taken if targets is None else jnp.where((lane8 & 3) == number, taken, targets)
    slot_row, slot_lane = inverse(targets)
    sent = slot_row >= 0
    for copy in inputs[1:]:
        copy.wait()
    cam = []
    for number in range(12):
        value = jnp.full((8, 128), cam_ref[0, number], F32)
        for other in range(1, 4):
            value = jnp.where((slot_lane & 3) == other, cam_ref[other, number], value)
        cam.append(value)

    for block in range(8):
        spread[pl.ds(block, 59, stride=8), :] = gauss_ref[:, block * 128 : block * 128 + 128]

    def read_params():
        return [spread[8 * number : 8 * number + 8, :] for number in range(59)]

    params = read_params()
    splats, pull_back = jax.vjp(lambda values: project(values, cam), params)
    logit = params[10]
    splats = [*splats, jnp.minimum(logit, 0.0) - jnp.log1p(jnp.exp(-jnp.abs(logit)))]
    logit_slope = 1.0 / (1.0 + jnp.exp(logit))
    chosen = jnp.maximum(targets, 0)
    outgoing = lookup(splats, chosen >> 7, chosen & 127)

    stage(outgoing, there)
    prepared = prepare(ids_ref, list_ref, len_ref, cot_ref, work[1], work[0])

    pl.semaphore_wait(barrier, PLANE - 1 + 2 * NEAR)
    for step, (_, device) in zip(Z_STEPS, z_partners):
        if ring(step, DEPTH) == NEAR:
            pl.semaphore_signal(far_sem, inc=1, device_id=device, device_id_type=MESH)
    arrived = exchange(where_am_i, there, between=lambda: pl.semaphore_wait(far_sem, 2))
    slot_grads = render(arrived, prepared, image_ref, *work)
    stage(slot_grads, back)
    returned = exchange(where_am_i, back)

    grads = lookup(returned, slot_row, slot_lane, jnp.zeros((8, 128), F32))
    (param_grads,) = pull_back(tuple(grads[0:8]))
    for number, value in enumerate(param_grads):
        if number == 10:
            value = grads[8] * logit_slope
        spread[8 * number : 8 * number + 8, :] = jnp.where(sent, value, 0.0)
    for block in range(8):
        out_ref[:, block * 128 : block * 128 + 128] = spread[pl.ds(block, 59, stride=8), :]


def store(image_ref, grads_ref, image_out, grads_out, sems):
    copies = [
        pltpu.make_async_copy(grads_ref, grads_out, sems.at[0]),
        pltpu.make_async_copy(image_ref.at[pl.ds(0, 3)], image_out, sems.at[1]),
    ]
    for copy in copies:
        copy.start()
    for copy in copies:
        copy.wait()


def exchange_scratch():
    return [
        pltpu.VMEM((DEPTH + 1, 8, 128), F32),
        pltpu.VMEM((PLANE + 2, 4, 128), F32),
        pltpu.VMEM((PLANE + 2, 4, 128), F32),
        pltpu.VMEM((DEPTH, 8, 128), F32),
        pltpu.VMEM((256, 128), F32),
        pltpu.SemaphoreType.DMA,
        pltpu.SemaphoreType.DMA,
        pltpu.SemaphoreType.DMA,
        pltpu.SemaphoreType.DMA,
    ]


def render_scratch():
    return [
        pltpu.VMEM((256, 128), F32),
        pltpu.VMEM((40, 256), F32),
        pltpu.VMEM((512, 256), F32),
        pltpu.VMEM((512, 256), F32),
        pltpu.VMEM((512, 256), F32),
        pltpu.VMEM((512, 256), F32),
        pltpu.VMEM((512, 256), BF16),
        pltpu.VMEM((512, 256), BF16),
        pltpu.VMEM((512, 256), F32),
        pltpu.VMEM((512, 256), BF16),
        pltpu.VMEM((512, 256), BF16),
        pltpu.VMEM((64, 128), F32),
        pltpu.VMEM((64, 128), F32),
    ]


def per_device(gaussians, camera, send_index, tile_ids, tile_lists, tile_lengths, pixel_grad):
    sends = jnp.transpose(send_index, (0, 1, 3, 2)).reshape(8, 128)
    lists = tile_lists.reshape(2, 256)
    vmem = pl.BlockSpec(memory_space=pltpu.VMEM)
    hbm = pl.BlockSpec(memory_space=pltpu.HBM)
    operands = [
        pltpu.with_memory_space_constraint(value, pltpu.HBM)
        for value in (gaussians, camera, sends, tile_ids, lists, tile_lengths, pixel_grad)
    ]
    results_shape = (
        jax.ShapeDtypeStruct((3, 1, 512), F32),
        jax.ShapeDtypeStruct((59, 1024), F32),
    )
    results = pl.pallas_call(
        kernel,
        out_shape=(
            jax.ShapeDtypeStruct((8, 1, 512), F32),
            jax.ShapeDtypeStruct((59, 1024), F32),
        ),
        in_specs=[hbm] * 7,
        out_specs=(vmem, vmem),
        scratch_shapes=[
            pltpu.VMEM((59, 1024), F32),
            pltpu.SMEM((4, 12), F32),
            pltpu.VMEM((8, 128), I32),
            pltpu.SMEM((1, 1, 2), I32),
            pltpu.VMEM((2, 256), I32),
            pltpu.SMEM((1, 1, 2), I32),
            pltpu.VMEM((8, 1, 512), F32),
            pltpu.SemaphoreType.DMA((7,)),
            pltpu.SemaphoreType.REGULAR,
            pltpu.VMEM((512, 128), F32),
            *exchange_scratch(),
            *exchange_scratch(),
            *render_scratch(),
        ],
        compiler_params=pltpu.CompilerParams(
            collective_id=0, has_side_effects=True, vmem_limit_bytes=32 * 1024 * 1024
        ),
    )(*operands)
    return tuple(
        pl.pallas_call(
            store,
            out_shape=results_shape,
            in_specs=[vmem, vmem],
            out_specs=(hbm, hbm),
            scratch_shapes=[pltpu.SemaphoreType.DMA((2,))],
            compiler_params=pltpu.CompilerParams(vmem_limit_bytes=1024 * 1024),
        )(*results)
    )


def solution(mesh):
    return jax.shard_map(
        per_device,
        mesh=mesh,
        in_specs=(
            P(None, ("tile", "view")),
            P(),
            P(("tile", "view"), None, None, None),
            P("view", "tile", None),
            P("view", "tile", None, None),
            P("view", "tile", None),
            P(None, "view", "tile"),
        ),
        out_specs=(P(None, "view", "tile"), P(None, ("tile", "view"))),
        check_vma=False,
    )
```

```python
import jax
import jax.numpy as jnp
from jax import lax
from jax.experimental import pallas as pl
from jax.experimental.pallas import tpu as pltpu
from jax.sharding import PartitionSpec as P

F32 = jnp.float32
BF16 = jnp.bfloat16
I32 = jnp.int32
MESH = pl.DeviceIdType.MESH
DEPTH = 16
NEAR = 4
PLANE = 32


def ring(distance, size):
    return min(distance, size - distance)


Z_STEPS = sorted(range(1, DEPTH), key=lambda step: -ring(step, DEPTH))
M_STEPS = sorted(
    [(x, core, y) for x in range(4) for core in range(2) for y in range(4) if x + core + y > 0],
    key=lambda step: -2 * (ring(step[0], 4) + ring(step[2], 4)) - step[1],
)


def project(params, cam):
    focal = 2400.0
    rotation = cam[:9]
    shift_x, shift_y, shift_z = cam[9:]
    world_x, world_y, world_z = params[0:3]
    view_x = rotation[0] * world_x + rotation[1] * world_y + rotation[2] * world_z + shift_x
    view_y = rotation[3] * world_x + rotation[4] * world_y + rotation[5] * world_z + shift_y
    depth = rotation[6] * world_x + rotation[7] * world_y + rotation[8] * world_z + shift_z
    scales = [jnp.exp(params[3 + number]) for number in range(3)]
    quat_real, quat_i, quat_j, quat_k = params[6:10]
    quat_inv = 1.0 / jnp.sqrt(
        quat_real * quat_real + quat_i * quat_i + quat_j * quat_j + quat_k * quat_k
    )
    quat_real = quat_real * quat_inv
    quat_i = quat_i * quat_inv
    quat_j = quat_j * quat_inv
    quat_k = quat_k * quat_inv
    spin = [
        [
            1.0 - 2.0 * (quat_j * quat_j + quat_k * quat_k),
            2.0 * (quat_i * quat_j - quat_real * quat_k),
            2.0 * (quat_i * quat_k + quat_real * quat_j),
        ],
        [
            2.0 * (quat_i * quat_j + quat_real * quat_k),
            1.0 - 2.0 * (quat_i * quat_i + quat_k * quat_k),
            2.0 * (quat_j * quat_k - quat_real * quat_i),
        ],
        [
            2.0 * (quat_i * quat_k - quat_real * quat_j),
            2.0 * (quat_j * quat_k + quat_real * quat_i),
            1.0 - 2.0 * (quat_i * quat_i + quat_j * quat_j),
        ],
    ]
    shaped = [[spin[row][col] * scales[col] for col in range(3)] for row in range(3)]
    depth_inv = 1.0 / depth
    inv_depth = focal * depth_inv
    screen_x = inv_depth * view_x
    screen_y = inv_depth * view_y
    slope_x = screen_x * depth_inv
    slope_y = screen_y * depth_inv
    jac_top = [inv_depth * rotation[col] - slope_x * rotation[6 + col] for col in range(3)]
    jac_low = [inv_depth * rotation[3 + col] - slope_y * rotation[6 + col] for col in range(3)]
    proj_top = [
        jac_top[0] * shaped[0][col] + jac_top[1] * shaped[1][col] + jac_top[2] * shaped[2][col]
        for col in range(3)
    ]
    proj_low = [
        jac_low[0] * shaped[0][col] + jac_low[1] * shaped[1][col] + jac_low[2] * shaped[2][col]
        for col in range(3)
    ]
    cov_xx = proj_top[0] * proj_top[0] + proj_top[1] * proj_top[1] + proj_top[2] * proj_top[2] + 0.3
    cov_xy = proj_top[0] * proj_low[0] + proj_top[1] * proj_low[1] + proj_top[2] * proj_low[2]
    cov_yy = proj_low[0] * proj_low[0] + proj_low[1] * proj_low[1] + proj_low[2] * proj_low[2] + 0.3
    det_inv = 1.0 / (cov_xx * cov_yy - cov_xy * cov_xy)
    conic_a = cov_yy * det_inv
    conic_b = -cov_xy * det_inv
    conic_c = cov_xx * det_inv
    centre_x = -(rotation[0] * shift_x + rotation[3] * shift_y + rotation[6] * shift_z)
    centre_y = -(rotation[1] * shift_x + rotation[4] * shift_y + rotation[7] * shift_z)
    centre_z = -(rotation[2] * shift_x + rotation[5] * shift_y + rotation[8] * shift_z)
    ray_x = world_x - centre_x
    ray_y = world_y - centre_y
    ray_z = world_z - centre_z
    ray_inv = 1.0 / jnp.sqrt(ray_x * ray_x + ray_y * ray_y + ray_z * ray_z)
    ray_x = ray_x * ray_inv
    ray_y = ray_y * ray_inv
    ray_z = ray_z * ray_inv
    sq_x = ray_x * ray_x
    sq_y = ray_y * ray_y
    sq_z = ray_z * ray_z
    basis = [
        -0.4886025119029199 * ray_y,
        0.4886025119029199 * ray_z,
        -0.4886025119029199 * ray_x,
        1.0925484305920792 * ray_x * ray_y,
        -1.0925484305920792 * ray_y * ray_z,
        0.31539156525252005 * (2.0 * sq_z - sq_x - sq_y),
        -1.0925484305920792 * ray_x * ray_z,
        0.5462742152960396 * (sq_x - sq_y),
        -0.5900435899266435 * ray_y * (3.0 * sq_x - sq_y),
        2.890611442640554 * ray_x * ray_y * ray_z,
        -0.4570457994644658 * ray_y * (4.0 * sq_z - sq_x - sq_y),
        0.3731763325901154 * ray_z * (2.0 * sq_z - 3.0 * sq_x - 3.0 * sq_y),
        -0.4570457994644658 * ray_x * (4.0 * sq_z - sq_x - sq_y),
        1.445305721320277 * ray_z * (sq_x - sq_y),
        -0.5900435899266435 * ray_x * (sq_x - 3.0 * sq_y),
    ]
    colours = []
    for channel in range(3):
        total = 0.5 + 0.28209479177387814 * params[11 + channel]
        for degree in range(1, 16):
            total = total + basis[degree - 1] * params[11 + 3 * degree + channel]
        colours.append(jnp.maximum(total, 0.0))
    return (screen_x + 1920.0, screen_y + 1080.0, conic_a, conic_b, conic_c, *colours)


def iotas(shape):
    return (lax.broadcasted_iota(I32, shape, 0), lax.broadcasted_iota(I32, shape, 1))


def take_lanes(values, lanes):
    return jnp.take_along_axis(
        jnp.broadcast_to(values, lanes.shape), lanes, axis=1, mode="promise_in_bounds"
    )


def lookup(tables, rows, lanes, start=None):
    results = [start] * len(tables)
    for row in range(tables[0].shape[0]):
        here = rows == row
        for number, table in enumerate(tables):
            taken = take_lanes(table[row : row + 1, :], lanes)
            if results[number] is None:
                results[number] = taken
            else:
                results[number] = jnp.where(here, taken, results[number])
    return results


def split2(values):
    high = values.astype(BF16).astype(F32)
    return (high, (values - high).astype(BF16).astype(F32))


def split3(values):
    high = values.astype(BF16).astype(F32)
    rest = values - high
    mid = rest.astype(BF16).astype(F32)
    return (high, mid, (rest - mid).astype(BF16).astype(F32))


def inverse(targets):
    count = targets.shape[0]
    target_row = targets >> 7
    target_lane = targets & 127
    sub8, _ = iotas((8, 128))
    sub128, _ = iotas((128, 128))
    lane = lax.broadcasted_iota(I32, (1, 128), 1).astype(F32)
    left, right = [], []
    for row in range(count):
        match = target_row[row : row + 1, :] == sub8
        low = jnp.where(match, lane, 0.0)
        high = jnp.where(match, float(row + 1), 0.0)
        left.append(jnp.concatenate([low, high], axis=0))
        right.append(jnp.where(target_lane[row : row + 1, :] == sub128, 1.0, 0.0))
    left = jnp.concatenate(left, axis=1).astype(BF16)
    right = jnp.concatenate(right, axis=1).astype(BF16)
    found = nt(left, right).astype(I32)
    return (found[8:16] - 1, found[0:8])


def nt(left, right):
    return lax.dot_general(
        left, right, (((1,), (1,)), ((), ())), preferred_element_type=F32
    )


def nn(left, right):
    return jnp.dot(left, right, preferred_element_type=F32)


def stage(values, bufs):
    packs = bufs[0]
    _, lane8 = iotas((8, 128))
    _, lane4 = iotas((4, 128))
    quarter8 = lane8 & 3
    for part in range(4):
        spot = part * 32 + (lane8 >> 2)
        for group in range(2):
            packed = take_lanes(values[4 * group], spot)
            for q in range(1, 4):
                packed = jnp.where(quarter8 == q, take_lanes(values[4 * group + q], spot), packed)
            for c in range(2):
                for plane in range(4):
                    row = 4 * c + plane
                    packs[4 * plane + part, pl.ds(2 * group + c, 1)] = packed[row : row + 1]
        last = take_lanes(values[8], spot)
        last = jnp.where((lane4 & 3) == 0, last[0:4], last[4:8])
        for plane in range(4):
            packs[4 * plane + part, pl.ds(4, 1)] = last[plane : plane + 1]


def exchange(where_am_i, bufs, meanwhile=lambda: None, between=lambda: None):
    my_z, my_m, z_partners, m_partners = where_am_i
    plane_out, plane_in, depth_out, depth_in, send1, recv1, send2, recv2 = bufs[1:]
    for to, device in m_partners:
        pltpu.make_async_remote_copy(
            src_ref=plane_out.at[to],
            dst_ref=plane_in.at[my_m],
            send_sem=send1,
            recv_sem=recv1,
            device_id=device,
            device_id_type=MESH,
        ).start()
    plane_in[my_m] = plane_out[my_m]
    meanwhile()
    plane_all = plane_in.at[pl.ds(0, PLANE - 1)]
    pltpu.make_async_copy(plane_all, plane_all, recv1).wait()
    depth_out[...] = plane_in[0:PLANE].reshape(128, 128).T.reshape(DEPTH, 8, 128)
    between()
    for to, device in z_partners:
        pltpu.make_async_remote_copy(
            src_ref=depth_out.at[to, pl.ds(0, 5)],
            dst_ref=depth_in.at[pl.ds(pl.multiple_of(my_z * 8, 8), 5)],
            send_sem=send2,
            recv_sem=recv2,
            device_id=device,
            device_id_type=MESH,
        ).start()
    depth_in[pl.ds(pl.multiple_of(my_z * 8, 8), 8), :] = depth_out[my_z]
    pltpu.make_async_copy(plane_all, plane_all, send1).wait()
    depth_all = depth_out.at[pl.ds(0, DEPTH - 1), pl.ds(0, 5)]
    pltpu.make_async_copy(depth_all, depth_all, recv2).wait()
    pltpu.make_async_copy(depth_all, depth_all, send2).wait()

    return unpack(depth_in)


def unpack(depth_in):
    sub8, lane8 = iotas((8, 128))
    part8 = lane8 >> 5
    base = (lane8 & 31) << 2
    results = []
    for group in range(2):
        blocks = [
            jnp.concatenate(
                [depth_in[pl.ds(part * 8 + 2 * group + c, 4, stride=32), :] for c in range(2)], axis=0
            )
            for part in range(4)
        ]
        for q in range(4):
            value = take_lanes(blocks[0], base + q)
            for part in range(1, 4):
                value = jnp.where(part8 == part, take_lanes(blocks[part], base + q), value)
            results.append(value)
    spot = base + (sub8 >> 2)
    value = None
    for part in range(4):
        block = depth_in[pl.ds(part * 8 + 4, 4, stride=32), :]
        taken = take_lanes(jnp.concatenate([block, block], axis=0), spot)
        value = taken if value is None else jnp.where(part8 == part, taken, value)
    results.append(value)
    return results


def exchange_back(where_am_i, bufs):
    my_z, my_m, z_partners, m_partners = where_am_i
    packs, plane_out, plane_in, planes, depth_in, send1, recv1, send2, recv2 = bufs
    for to, device in z_partners:
        pltpu.make_async_remote_copy(
            src_ref=packs.at[to, pl.ds(0, 5)],
            dst_ref=planes.at[my_z, pl.ds(0, 5)],
            send_sem=send2,
            recv_sem=recv2,
            device_id=device,
            device_id_type=MESH,
        ).start()
    planes[my_z] = packs[my_z]
    planes_all = planes.at[pl.ds(0, DEPTH - 1), pl.ds(0, 5)]
    pltpu.make_async_copy(planes_all, planes_all, recv2).wait()
    plane_out[0:PLANE] = planes[...].reshape(128, 128).T.reshape(PLANE, 4, 128)
    for to, device in m_partners:
        pltpu.make_async_remote_copy(
            src_ref=plane_out.at[to],
            dst_ref=plane_in.at[my_m],
            send_sem=send1,
            recv_sem=recv1,
            device_id=device,
            device_id_type=MESH,
        ).start()
    plane_in[my_m] = plane_out[my_m]
    pltpu.make_async_copy(planes_all, planes_all, send2).wait()
    plane_all = plane_in.at[pl.ds(0, PLANE - 1)]
    pltpu.make_async_copy(plane_all, plane_all, recv1).wait()
    depth_in[0:128, :] = plane_in[0:PLANE].reshape(128, 128).T
    pltpu.make_async_copy(plane_all, plane_all, send1).wait()
    return unpack(depth_in)


def prepare(ids_ref, list_ref, len_ref, cot_ref, colour_s, coef_s):
    sub4, lane4 = iotas((4, 128))
    low = jnp.concatenate([list_ref[t : t + 1, 0:128] for t in (0, 0, 1, 1)], axis=0)
    high = jnp.concatenate([list_ref[t : t + 1, 128:256] for t in (0, 0, 1, 1)], axis=0)
    spot = 32 * (lane4 & 3) + (sub4 & 1) * 16 + (lane4 >> 3)
    slots = jnp.where((lane4 & 7) < 4, take_lanes(low, spot), take_lanes(high, spot))
    entry = 32 * (lane4 & 7) + (sub4 & 1) * 16 + (lane4 >> 3)
    live = entry < jnp.where(sub4 < 2, len_ref[0, 0, 0], len_ref[0, 0, 1])
    back_row, back_lane = inverse(jnp.where(live, slots, -1))

    first_x = (ids_ref[0, 0, 0] % 240 * 16).astype(F32) + 7.5
    first_y = (ids_ref[0, 0, 0] // 240 * 16).astype(F32) + 7.5
    other_x = (ids_ref[0, 0, 1] % 240 * 16).astype(F32) + 7.5
    other_y = (ids_ref[0, 0, 1] // 240 * 16).astype(F32) + 7.5
    corner = (jnp.where(sub4 < 2, first_x, other_x), jnp.where(sub4 < 2, first_y, other_y))
    colour_s[...] = jnp.zeros_like(colour_s)
    for row in (30, 31):
        coef_s[pl.ds(row, 4, stride=32), :] = jnp.zeros((4, 128), F32)
    row32, pixel = iotas((32, 256))
    local_x = (pixel & 15).astype(F32) - 7.5
    local_y = (pixel >> 4).astype(F32) - 7.5
    terms = [
        local_x * local_x,
        local_y * local_y,
        local_x * local_y,
        local_x,
        local_y,
        jnp.ones_like(local_x),
    ]
    basis = jnp.zeros_like(local_x)
    moments = jnp.zeros_like(local_x)
    for number, term in enumerate(terms):
        basis = jnp.where((row32 >= 3 * number) & (row32 < 3 * number + 3), term, basis)
        moments = jnp.where(row32 == number, term, moments)
    basis = basis.astype(BF16)
    moments = moments[0:16].astype(BF16)
    cot_rows, shades = [], []
    for t in range(2):
        shade = jnp.zeros_like(local_x)
        sums = jnp.zeros_like(local_x)
        for channel in range(3):
            value = cot_ref[channel, 0:1, t * 256 : t * 256 + 256]
            piece_h, piece_l = split2(value)
            start = 18 + 4 * channel
            shade = jnp.where((row32 == start) | (row32 == start + 2), piece_h, shade)
            shade = jnp.where((row32 == start + 1) | (row32 == start + 3), piece_l, shade)
            sums = jnp.where(row32 == channel, piece_h, sums)
            sums = jnp.where(row32 == channel + 8, piece_l, sums)
        cot_rows.append(sums[0:16].astype(BF16))
        shades.append(shade.astype(BF16))
    return (live, slots >> 7, slots & 127, back_row, back_lane, corner, basis, moments, cot_rows, shades)


def render(
    table, prepared, image_ref,
    coef_s, colour_s, power_s, shade_s, alpha_s, keep_s, weight_h, weight_l, after_s, grad_h, grad_l, sum_s, tint_s,
):
    live, slot_row, slot_lane, back_row, back_lane, corner, basis, moments, cot_rows, shades = prepared
    pos_x, pos_y, con_a, con_b, con_c, red, green, blue, log_o = lookup(table, slot_row, slot_lane)
    pos_x = pos_x - corner[0]
    pos_y = pos_y - corner[1]
    slope_x = con_a * pos_x + con_b * pos_y
    slope_y = con_c * pos_y + con_b * pos_x
    level = log_o - 0.5 * (slope_x * pos_x + slope_y * pos_y)
    coefs = [-0.5 * con_a, -0.5 * con_c, -con_b, slope_x, slope_y]
    coefs = [jnp.where(live, value, 0.0) for value in coefs]
    coefs.append(jnp.where(live, level, -1.0e5))
    for number, value in enumerate(coefs):
        for part, piece in enumerate(split3(value)):
            coef_s[pl.ds(3 * number + part, 4, stride=32), :] = piece
    for channel, value in enumerate((red, green, blue)):
        piece_h, piece_l = split2(value)
        for part in range(4):
            coef_s[pl.ds(18 + 4 * channel + part, 4, stride=32), :] = (piece_h, piece_l)[part // 2]
        for block in range(4):
            cols = slice((block % 2) * 128, (block % 2) * 128 + 128)
            at = block // 2 * 16 + channel
            colour_s[at : at + 1, cols] = piece_h[block : block + 1, :]
            colour_s[at + 8 : at + 9, cols] = piece_l[block : block + 1, :]

    for t in range(2):
        left = jnp.concatenate(
            [coef_s[(2 * t + h) * 32 : (2 * t + h) * 32 + 32, :].T for h in range(2)], axis=0
        ).astype(BF16)
        power_s[t * 256 : t * 256 + 256, :] = nn(left, basis)
        shade_s[t * 256 : t * 256 + 256, :] = nn(left, shades[t])

    sub_k, _ = iotas((8, 256))

    def ahead(values):
        result = jnp.where(sub_k >= 1, pltpu.roll(values, 1, 0), 1.0)
        for shift in (1, 2, 4):
            result = result * jnp.where(sub_k >= shift, pltpu.roll(result, shift, 0), 1.0)
        return result

    def behind(values):
        result = jnp.where(sub_k < 7, pltpu.roll(values, 7, 0), 0.0)
        for shift in (1, 2, 4):
            result = result + jnp.where(sub_k < 8 - shift, pltpu.roll(result, 8 - shift, 0), 0.0)
        return result

    def forward(t):
        kept = jnp.ones((8, 256), F32)
        for block in range(32):
            rows = slice(t * 256 + block * 8, t * 256 + block * 8 + 8)
            alpha = jnp.exp(power_s[rows, :])
            alpha_s[rows, :] = alpha
            keep_s[rows, :] = kept
            kept = kept * (1.0 - alpha)
        return ahead(kept)

    def backward(t, entering):
        total = jnp.zeros((8, 256), F32)
        for pair in reversed(range(16)):
            start = t * 256 + pair * 16
            weights = [None, None]
            for half in (1, 0):
                rows = slice(start + half * 8, start + half * 8 + 8)
                weight = keep_s[rows, :] * entering * alpha_s[rows, :]
                gain = weight * shade_s[rows, :]
                weights[half] = weight
                after_s[rows, :] = total
                power_s[rows, :] = gain
                total = total + gain
            weight = jnp.concatenate(weights, axis=0)
            rows = slice(start, start + 16)
            piece = weight.astype(BF16)
            weight_h[rows, :] = piece
            weight_l[rows, :] = (weight - piece.astype(F32)).astype(BF16)
        return behind(total)

    def slopes(t, leaving):
        leaving = jnp.concatenate([leaving, leaving], axis=0)
        for pair in range(16):
            rows = slice(t * 256 + pair * 16, t * 256 + pair * 16 + 16)
            alpha = alpha_s[rows, :]
            ratio = alpha / (1.0 - alpha)
            grad = power_s[rows, :] - ratio * (after_s[rows, :] + leaving)
            piece = grad.astype(BF16)
            grad_h[rows, :] = piece
            grad_l[rows, :] = (grad - piece.astype(F32)).astype(BF16)

    def paint(t):
        rows = slice(t * 256, t * 256 + 256)
        tints = colour_s[t * 16 : t * 16 + 16, :].astype(BF16)
        picture = nn(tints, weight_h[rows, :]) + nn(tints, weight_l[rows, :])
        picture = picture[0:8] + picture[8:16]
        for channel in range(3):
            image_ref[channel, 0:1, rows] = picture[channel : channel + 1, :]
        tint = nt(cot_rows[t], weight_h[rows, :]) + nt(cot_rows[t], weight_l[rows, :])
        tint = tint[0:8] + tint[8:16]
        for h in range(2):
            at = (2 * t + h) * 8
            tint_s[at : at + 8, :] = tint[:, h * 128 : h * 128 + 128]

    def gather_moments(t):
        rows = slice(t * 256, t * 256 + 256)
        total = nt(moments, grad_h[rows, :]) + nt(moments, grad_l[rows, :])
        for h in range(2):
            at = (2 * t + h) * 8
            sum_s[at : at + 8, :] = total[0:8, h * 128 : h * 128 + 128]

    entering = [forward(t) for t in range(2)]
    leaving = []
    for t in range(2):
        leaving.append(backward(t, entering[t]))
        paint(t)
    for t in range(2):
        slopes(t, leaving[t])
        gather_moments(t)
    sum_xx, sum_yy, sum_xy, sum_x, sum_y, sum_1 = [
        sum_s[pl.ds(number, 4, stride=8), :] for number in range(6)
    ]
    tints = [tint_s[pl.ds(number, 4, stride=8), :] for number in range(3)]
    first_mx = sum_x - pos_x * sum_1
    first_my = sum_y - pos_y * sum_1
    grads = [
        con_a * first_mx + con_b * first_my,
        con_c * first_my + con_b * first_mx,
        -0.5 * (sum_xx - pos_x * (sum_x + first_mx)),
        -(sum_xy - pos_x * sum_y - pos_y * first_mx),
        -0.5 * (sum_yy - pos_y * (sum_y + first_my)),
        *tints,
        sum_1,
    ]
    return lookup(grads, back_row, back_lane, jnp.zeros((8, 128), F32))


def kernel(
    gauss_hbm, cam_hbm, send_hbm, ids_hbm, list_hbm, len_hbm, cot_hbm, image_ref, out_ref,
    gauss_ref, cam_ref, send_ref, ids_ref, list_ref, len_ref, cot_ref, in_sem, far_sem, spread, *scratch,
):
    there, back, work = scratch[0:9], scratch[9:18], scratch[18:]
    tile = lax.axis_index("tile")
    view = lax.axis_index("view")
    my_z = tile // 8
    mine = lax.rem(tile, 8)
    my_x, my_core = mine // 2, lax.rem(mine, 2)
    my_m = mine * 4 + view
    z_partners, m_partners = [], []
    for step in Z_STEPS:
        to = lax.rem(my_z + step, DEPTH)
        z_partners.append((to, (to * 8 + mine, view)))
    for x, core, y in M_STEPS:
        place = lax.rem(my_x + x, 4) * 2 + lax.rem(my_core + core, 2)
        row = lax.rem(view + y, 4)
        m_partners.append((place * 4 + row, (my_z * 8 + place, row)))
    where_am_i = (my_z, my_m, z_partners, m_partners)

    barrier = pltpu.get_barrier_semaphore()

    near = [entry for step, entry in zip(Z_STEPS, z_partners) if ring(step, DEPTH) <= NEAR]
    for _, device in near + m_partners:
        pl.semaphore_signal(barrier, inc=1, device_id=device, device_id_type=MESH)

    inputs = [
        pltpu.make_async_copy(source, target, in_sem.at[number])
        for number, (source, target) in enumerate(
            [
                (send_hbm, send_ref),
                (gauss_hbm, gauss_ref),
                (cam_hbm, cam_ref),
                (ids_hbm, ids_ref),
                (list_hbm, list_ref),
                (len_hbm, len_ref),
                (cot_hbm, cot_ref.at[pl.ds(0, 3)]),
            ]
        )
    ]
    for copy in inputs:
        copy.start()
    inputs[0].wait()

    sub8, lane8 = iotas((8, 128))
    spot = (sub8 & 3) * 32 + (lane8 >> 2)
    targets = None
    for number in range(4):
        row = jnp.where(sub8 < 4, send_ref[number : number + 1, :], send_ref[4 + number : 5 + number, :])
        taken = take_lanes(row, spot)
        targets = taken if targets is None else jnp.where((lane8 & 3) == number, taken, targets)
    slot_row, slot_lane = inverse(targets)
    sent = slot_row >= 0
    for copy in inputs[1:]:
        copy.wait()
    cam = []
    for number in range(12):
        value = jnp.full((8, 128), cam_ref[0, number], F32)
        for other in range(1, 4):
            value = jnp.where((slot_lane & 3) == other, cam_ref[other, number], value)
        cam.append(value)

    for block in range(8):
        spread[pl.ds(block, 59, stride=8), :] = gauss_ref[:, block * 128 : block * 128 + 128]

    def read_params():
        return [spread[8 * number : 8 * number + 8, :] for number in range(59)]

    params = read_params()
    splats, pull_back = jax.vjp(lambda values: project(values, cam), params)
    logit = params[10]
    splats = [*splats, jnp.minimum(logit, 0.0) - jnp.log1p(jnp.exp(-jnp.abs(logit)))]
    logit_slope = 1.0 / (1.0 + jnp.exp(logit))
    chosen = jnp.maximum(targets, 0)
    outgoing = lookup(splats, chosen >> 7, chosen & 127)

    stage(outgoing, there)
    there[1][0:PLANE] = there[0][0:DEPTH].reshape(128, 128).T.reshape(PLANE, 4, 128)
    prepared = prepare(ids_ref, list_ref, len_ref, cot_ref, work[1], work[0])

    pl.semaphore_wait(barrier, PLANE - 1 + 2 * NEAR)
    for step, (_, device) in zip(Z_STEPS, z_partners):
        if ring(step, DEPTH) == NEAR:
            pl.semaphore_signal(far_sem, inc=1, device_id=device, device_id_type=MESH)
    arrived = exchange(where_am_i, there, between=lambda: pl.semaphore_wait(far_sem, 2))
    slot_grads = render(arrived, prepared, image_ref, *work)
    stage(slot_grads, back)
    returned = exchange_back(where_am_i, back)

    grads = lookup(returned, slot_row, slot_lane, jnp.zeros((8, 128), F32))
    (param_grads,) = pull_back(tuple(grads[0:8]))
    for number, value in enumerate(param_grads):
        if number == 10:
            value = grads[8] * logit_slope
        spread[8 * number : 8 * number + 8, :] = jnp.where(sent, value, 0.0)
    for block in range(8):
        out_ref[:, block * 128 : block * 128 + 128] = spread[pl.ds(block, 59, stride=8), :]


def store(image_ref, grads_ref, image_out, grads_out, sems):
    copies = [
        pltpu.make_async_copy(grads_ref, grads_out, sems.at[0]),
        pltpu.make_async_copy(image_ref.at[pl.ds(0, 3)], image_out, sems.at[1]),
    ]
    for copy in copies:
        copy.start()
    for copy in copies:
        copy.wait()


def exchange_scratch():
    return [
        pltpu.VMEM((DEPTH + 1, 8, 128), F32),
        pltpu.VMEM((PLANE + 2, 4, 128), F32),
        pltpu.VMEM((PLANE + 2, 4, 128), F32),
        pltpu.VMEM((DEPTH, 8, 128), F32),
        pltpu.VMEM((256, 128), F32),
        pltpu.SemaphoreType.DMA,
        pltpu.SemaphoreType.DMA,
        pltpu.SemaphoreType.DMA,
        pltpu.SemaphoreType.DMA,
    ]


def render_scratch():
    return [
        pltpu.VMEM((256, 128), F32),
        pltpu.VMEM((40, 256), F32),
        pltpu.VMEM((512, 256), F32),
        pltpu.VMEM((512, 256), F32),
        pltpu.VMEM((512, 256), F32),
        pltpu.VMEM((512, 256), F32),
        pltpu.VMEM((512, 256), BF16),
        pltpu.VMEM((512, 256), BF16),
        pltpu.VMEM((512, 256), F32),
        pltpu.VMEM((512, 256), BF16),
        pltpu.VMEM((512, 256), BF16),
        pltpu.VMEM((64, 128), F32),
        pltpu.VMEM((64, 128), F32),
    ]


def per_device(gaussians, camera, send_index, tile_ids, tile_lists, tile_lengths, pixel_grad):
    sends = jnp.transpose(send_index, (0, 1, 3, 2)).reshape(8, 128)
    lists = tile_lists.reshape(2, 256)
    vmem = pl.BlockSpec(memory_space=pltpu.VMEM)
    hbm = pl.BlockSpec(memory_space=pltpu.HBM)
    operands = [
        pltpu.with_memory_space_constraint(value, pltpu.HBM)
        for value in (gaussians, camera, sends, tile_ids, lists, tile_lengths, pixel_grad)
    ]
    results_shape = (
        jax.ShapeDtypeStruct((3, 1, 512), F32),
        jax.ShapeDtypeStruct((59, 1024), F32),
    )
    results = pl.pallas_call(
        kernel,
        out_shape=(
            jax.ShapeDtypeStruct((8, 1, 512), F32),
            jax.ShapeDtypeStruct((59, 1024), F32),
        ),
        in_specs=[hbm] * 7,
        out_specs=(vmem, vmem),
        scratch_shapes=[
            pltpu.VMEM((59, 1024), F32),
            pltpu.SMEM((4, 12), F32),
            pltpu.VMEM((8, 128), I32),
            pltpu.SMEM((1, 1, 2), I32),
            pltpu.VMEM((2, 256), I32),
            pltpu.SMEM((1, 1, 2), I32),
            pltpu.VMEM((8, 1, 512), F32),
            pltpu.SemaphoreType.DMA((7,)),
            pltpu.SemaphoreType.REGULAR,
            pltpu.VMEM((512, 128), F32),
            *exchange_scratch(),
            *exchange_scratch(),
            *render_scratch(),
        ],
        compiler_params=pltpu.CompilerParams(
            collective_id=0, has_side_effects=True, vmem_limit_bytes=32 * 1024 * 1024
        ),
    )(*operands)
    return tuple(
        pl.pallas_call(
            store,
            out_shape=results_shape,
            in_specs=[vmem, vmem],
            out_specs=(hbm, hbm),
            scratch_shapes=[pltpu.SemaphoreType.DMA((2,))],
            compiler_params=pltpu.CompilerParams(vmem_limit_bytes=1024 * 1024),
        )(*results)
    )


def solution(mesh):
    return jax.shard_map(
        per_device,
        mesh=mesh,
        in_specs=(
            P(None, ("tile", "view")),
            P(),
            P(("tile", "view"), None, None, None),
            P("view", "tile", None),
            P("view", "tile", None, None),
            P("view", "tile", None),
            P(None, "view", "tile"),
        ),
        out_specs=(P(None, "view", "tile"), P(None, ("tile", "view"))),
        check_vma=False,
    )
```
